512 devices in a mesh: grp: 8 (over y), row: 8 (over z), col: 8 (over x, core).
Axes of the slice: x: 4, y: 8, z: 8, core: 2. Of those that a mesh axis runs over, the one named last changes fastest.
Arguments:
- new_rows: bfloat16 [768, 16, 8192], P(('grp', 'col'), None, 'row'), may hold values from -6 to 6
- query_weight: bfloat16 [8192, 8192], P('row', 'col')
- key_weight: bfloat16 [8192, 1024], P('row', 'col')
- value_weight: bfloat16 [8192, 1024], P('row', 'col'), may hold values from -0.0625 to 0.0625
- cache_keys: bfloat16 [768, 512, 1024], P(('grp', 'row'), None, 'col'), may hold values from -6 to 6
- cache_values: bfloat16 [768, 512, 1024], P(('grp', 'row'), None, 'col'), may hold values from -6 to 6
- region_agents: int32 [768], replicated, may hold values from 0 to 767, as said below
- new_counts: int32 [768], replicated, may hold values from 4 to 16, as said below
- cache_lengths: int32 [768], replicated, may hold values from 1 to 512, as said below
Outputs:
- attended: bfloat16 [768, 16, 8192], P(('grp', 'col'), 'row')
The draws below stay inside these ranges and needn't reach their ends.
Inputs may be any that keep to these rules, and one draw needn't show every extreme that they name: `region_agents`: A permutation of the 768 agents. Rows i with equal i // 12 form one region; agent a is served by group a // 96. Every region holds at most 3 agents served by one group, and exactly 3 of some group. `new_counts`: some agent has 16 new tokens. `cache_lengths`: some agent has 512 cached positions.
All inputs are finite; a program needn't handle non-finite values.
Results may differ from the reference program's by a relative error of at most 0.025.
Values may be sent and summed in bfloat16 or wider, within the bound.
A program may use at most 64 MiB of HBM per device.

```python
import jax
import jax.numpy as jnp
from jax import lax

D = 8192
HEADS = 64
KV_HEADS = 8
HEAD_DIM = 128
NEW_MAX = 16
CACHE_MAX = 512
AG_GRP = 96
AGENTS = 768
BUCKET = 3
N_GRP = 8
N_ROW = 8
N_COL = 8


def shared_key_weight(key):
    return jax.random.normal(jax.random.fold_in(key, 11), (D, KV_HEADS * HEAD_DIM), jnp.float32) * D ** (-0.5)


def draw_key_weight(key, part):
    return shared_key_weight(key).astype(jnp.bfloat16)


def draw_query_weight(key, part):
    fresh_weight = jax.random.normal(jax.random.fold_in(key, 12), (D, HEADS * HEAD_DIM), jnp.float32) * D ** (-0.5)
    return fresh_weight.astype(jnp.bfloat16)


def draw_new_counts(key, part):
    counts = jax.random.randint(jax.random.fold_in(key, 21), (AGENTS,), 4, NEW_MAX + 1)
    chosen = jax.random.randint(jax.random.fold_in(key, 22), (), 0, AGENTS)
    return counts.at[chosen].set(NEW_MAX).astype(jnp.int32)


def draw_cache_lengths(key, part):
    root_value = jax.random.randint(jax.random.fold_in(key, 31), (AGENTS,), 1, 33)
    lengths = jnp.maximum(root_value * root_value * CACHE_MAX // 1024, 1)
    chosen = jax.random.randint(jax.random.fold_in(key, 32), (), 0, AGENTS)
    return lengths.at[chosen].set(CACHE_MAX).astype(jnp.int32)


def draw_region_agents(key, part):
    groups = N_GRP
    grid_cols = N_COL
    per_group = AG_GRP
    per_region = per_group // grid_cols
    regions = groups * grid_cols
    bucket_cap = BUCKET
    remaining = per_region - bucket_cap
    others = groups - 1
    tail_slots = jnp.arange(others, dtype=jnp.int32)
    even_split = remaining // others + (tail_slots < remaining % others).astype(jnp.int32)
    tail_counts = jnp.broadcast_to(even_split[None, :], (grid_cols, others))
    column_ids = jnp.arange(grid_cols)
    giver_index = jax.random.randint(jax.random.fold_in(key, 41), (grid_cols,), 0, others)
    offset_draw = jax.random.randint(jax.random.fold_in(key, 42), (grid_cols,), 0, others)
    taker_index = (giver_index + 1 + offset_draw) % others
    headroom = jnp.minimum(tail_counts[column_ids, giver_index], bucket_cap - tail_counts[column_ids, taker_index])
    moved_units = jax.random.randint(jax.random.fold_in(key, 43), (grid_cols,), 0, 1 << 20) % (headroom + 1)
    tail_counts = tail_counts - moved_units[:, None] * (tail_slots[None, :] == giver_index[:, None]) + moved_units[:, None] * (tail_slots[None, :] == taker_index[:, None])
    tail_order = jax.vmap(lambda subkey: jax.random.permutation(subkey, others))(jax.random.split(jax.random.fold_in(key, 44), grid_cols))
    tail_counts = jnp.take_along_axis(tail_counts, tail_order, axis=1)
    vector = jnp.concatenate([jnp.full((grid_cols, 1), bucket_cap, jnp.int32), tail_counts.astype(jnp.int32)], axis=1)
    shift_amount = jax.random.randint(jax.random.fold_in(key, 45), (grid_cols,), 0, groups)
    region_ids = jnp.arange(regions)
    region_grp = region_ids // grid_cols
    region_col = region_ids % grid_cols
    target = jnp.arange(groups)
    lookup = (target[None, :] - region_grp[:, None] - shift_amount[region_col][:, None]) % groups
    counts = jnp.take_along_axis(vector[region_col], lookup, axis=1)
    bounds = jnp.cumsum(counts, axis=0)
    group_ranks = jax.vmap(lambda subkey: jax.random.permutation(subkey, per_group))(jax.random.split(jax.random.fold_in(key, 46), groups))
    region_of = jnp.sum((bounds[:, :, None] <= group_ranks[None, :, :]).astype(jnp.int32), axis=0)
    tiebreak = jax.random.permutation(jax.random.fold_in(key, 47), regions * per_region)
    ordering = region_of.reshape(-1) * (regions * per_region) + tiebreak
    return jnp.argsort(ordering, stable=True).astype(jnp.int32)


def shard_levels(stream_key, shape, cuts, low, largest):
    factor_of = 1.0
    for position, blocks in cuts:
        draws = jax.random.uniform(jax.random.fold_in(jax.random.fold_in(stream_key, 6), position), (blocks,), jnp.float32, low / len(cuts), largest / len(cuts))
        factor_of = factor_of * jnp.repeat(jnp.exp(draws), shape[position] // blocks).reshape((-1,) + (1,) * (len(shape) - 1 - position))
    return factor_of


def normal_values(own_key, shape, deviation, most, pieces=(), held_as=jnp.bfloat16):
    array = deviation * jax.random.normal(own_key, shape, jnp.float32)
    if pieces:
        array = array * shard_levels(own_key, shape, pieces, -0.22, 0.18)
    return jnp.clip(array, -most, most).astype(held_as)


def setup_inputs(seed: int = 0) -> dict:
    key_of = jax.random.split(jax.random.key(seed), 10)
    new_rows = normal_values(key_of[0], (AGENTS, NEW_MAX, D), 1.0, 6.0, ((0, 64), (2, 8)))
    query_weight = draw_query_weight(jax.random.fold_in(key_of[9], 71), 0)
    key_weight = draw_key_weight(jax.random.fold_in(key_of[9], 71), 0)
    value_weight = normal_values(key_of[3], (D, KV_HEADS * HEAD_DIM), D ** -0.5, 0.0625, ((0, 8), (1, 8)))
    cache_keys = normal_values(key_of[4], (AGENTS, CACHE_MAX, KV_HEADS * HEAD_DIM), 1.0, 6.0, ((0, 64), (2, 8)))
    cache_values = normal_values(key_of[5], (AGENTS, CACHE_MAX, KV_HEADS * HEAD_DIM), 1.0, 6.0, ((0, 64), (2, 8)))
    region_agents = draw_region_agents(jax.random.fold_in(key_of[9], 71), 0)
    new_counts = draw_new_counts(jax.random.fold_in(key_of[9], 71), 0)
    cache_lengths = draw_cache_lengths(jax.random.fold_in(key_of[9], 71), 0)
    return {"new_rows": new_rows, "query_weight": query_weight, "key_weight": key_weight, "value_weight": value_weight, "cache_keys": cache_keys, "cache_values": cache_values, "region_agents": region_agents, "new_counts": new_counts, "cache_lengths": cache_lengths}


rotary_base = 500000.0


def rotate_pairs(values, positions):
    half_dim = values.shape[-1] // 2
    exponent = jnp.arange(half_dim, dtype=jnp.float32) * (2.0 / values.shape[-1])
    frequency = rotary_base ** (-exponent)
    angles = positions.astype(jnp.float32)[..., None, None] * frequency
    cosine = jnp.cos(angles)
    sine_part = jnp.sin(angles)
    first_half = values[..., :half_dim]
    second = values[..., half_dim:]
    return jnp.concatenate([first_half * cosine - second * sine_part, second * cosine + first_half * sine_part], axis=-1)


def block_product(flat_rows, weight):
    block_width = flat_rows.shape[1] // N_ROW
    summed_total = jnp.zeros((flat_rows.shape[0], weight.shape[1]), jnp.float32)
    for block_index in range(N_ROW):
        lower = block_index * block_width
        partial_sum = jnp.dot(flat_rows[:, lower:lower + block_width], weight[lower:lower + block_width], preferred_element_type=jnp.float32)
        rounded = lax.optimization_barrier(partial_sum.astype(jnp.bfloat16))
        summed_total = summed_total + rounded.astype(jnp.float32)
    return summed_total


def reference(new_rows, query_weight, key_weight, value_weight, cache_keys, cache_values, region_agents, new_counts, cache_lengths):
    group_ratio = HEADS // KV_HEADS
    slot_of_agent = jnp.argsort(region_agents).astype(jnp.int32)
    rows_of_agent = jnp.take(new_rows, slot_of_agent, axis=0)
    flat_rows = rows_of_agent.reshape(AGENTS * NEW_MAX, D)
    positions = cache_lengths[:, None] + jnp.arange(NEW_MAX, dtype=jnp.int32)[None, :]
    query_raw = block_product(flat_rows, query_weight).reshape(AGENTS, NEW_MAX, HEADS, HEAD_DIM)
    key_raw = block_product(flat_rows, key_weight).reshape(AGENTS, NEW_MAX, KV_HEADS, HEAD_DIM)
    value_raw = block_product(flat_rows, value_weight).reshape(AGENTS, NEW_MAX, KV_HEADS, HEAD_DIM)
    queries = rotate_pairs(query_raw, positions).astype(jnp.bfloat16)
    fresh_keys = rotate_pairs(key_raw, positions).astype(jnp.bfloat16)
    fresh_values = value_raw.astype(jnp.bfloat16)

    def attend_agent(inputs):
        query_one, key_one, value_one, stored_keys, stored_values, length_one, count_one = inputs
        keys_all = jnp.concatenate([stored_keys.reshape(CACHE_MAX, KV_HEADS, HEAD_DIM), key_one], axis=0).astype(jnp.float32)
        values_all = jnp.concatenate([stored_values.reshape(CACHE_MAX, KV_HEADS, HEAD_DIM), value_one], axis=0).astype(jnp.float32)
        grouped = query_one.reshape(NEW_MAX, KV_HEADS, group_ratio, HEAD_DIM).astype(jnp.float32)
        scores = jnp.einsum("skrd,pkd->krsp", grouped, keys_all) * (HEAD_DIM ** -0.5)
        key_index = jnp.arange(CACHE_MAX + NEW_MAX, dtype=jnp.int32)
        slot_index = jnp.arange(NEW_MAX, dtype=jnp.int32)
        fresh_index = key_index - CACHE_MAX
        cached_ok = (key_index < length_one)[None, :]
        fresh_ok = (fresh_index[None, :] <= slot_index[:, None]) & (fresh_index[None, :] < count_one)
        allowed = jnp.where(key_index[None, :] < CACHE_MAX, cached_ok, fresh_ok)
        masked = jnp.where(allowed[None, None], scores, -jnp.inf)
        row_max = jnp.max(masked, axis=3, keepdims=True)
        probs = jnp.where(allowed[None, None], jnp.exp(masked - row_max), 0.0)
        denominator = jnp.sum(probs, axis=3)
        probs_rounded = lax.optimization_barrier(probs.astype(jnp.bfloat16)).astype(jnp.float32)
        mixed = jnp.einsum("krsp,pkd->skrd", probs_rounded, values_all) / denominator.transpose(2, 0, 1)[..., None]
        mixed = jnp.where((slot_index < count_one)[:, None, None, None], mixed, 0.0)
        return mixed.reshape(NEW_MAX, HEADS * HEAD_DIM).astype(jnp.bfloat16)

    attended_agents = lax.map(attend_agent, (queries, fresh_keys, fresh_values, cache_keys, cache_values, cache_lengths, new_counts))
    return jnp.take(attended_agents, region_agents, axis=0)
```

```python
import jax
import jax.numpy as jnp
import numpy as np
from jax import lax
from jax.experimental import pallas as pl
from jax.experimental.pallas import tpu as pltpu
from jax.sharding import PartitionSpec as P

HEAD_DIM = 128
SLOTS = 16
CAP = 3
rotary_base = 500000.0
floor_score = -1e30
MESH = pl.DeviceIdType.MESH

GROUPS = (8,)
N_GROUPS = len(GROUPS)
N_ROW = 8
PLUS, MINUS = 0, 1
MESSAGES = ((1, 4), (0, 3), (1, 3), (0, 2), (1, 2), (0, 1), (1, 1))
OFFSETS = (4, 3, -3, 2, -2, 1, -1, 0)


def group_columns():
    found, at = [], 0
    for i, heads in enumerate(GROUPS):
        width = (heads + (2 if i == 0 else 0)) * HEAD_DIM
        found.append((at, width // 2))
        at += width
    return found


COLUMNS = group_columns()


def message_index(direction, half, distance):
    long = 1 if half == direction else 0
    return MESSAGES.index((long, distance))


def whole_wait(ref, sem):
    pltpu.make_async_copy(ref, ref, sem).wait()


def kernel(*refs):
    refs = list(refs)
    take = lambda n: [refs.pop(0) for _ in range(n)]
    idx, cosine, sine, rows, wq, wk, wv, keys, values = take(9)
    (out,) = take(1)
    outg, arrv, xg, wbuf, kbuf, vbuf, kn, vn = take(8)
    sbuf = [take(2) for _ in range(N_GROUPS)]
    rbuf = [take(2) for _ in range(N_GROUPS)]
    qs, zs, zr, bo, inc = (take(N_GROUPS) for _ in range(5))
    local_sem, d_send, d_recv, ag_send, ag_recv, rs_send, rs_recv, z_send, z_recv, b_send, b_recv = take(11)

    g = lax.axis_index("grp")
    r = lax.axis_index("row")
    c = lax.axis_index("col")
    me = g * 8 + c
    SEND, RECV, BACK, FING, FINK, LENS, CNTS = 0, 24, 120, 312, 324, 336, 348

    loads = [
        pltpu.make_async_copy(wk, wbuf.at[:, pl.ds(0, HEAD_DIM)], local_sem.at[0]),
        pltpu.make_async_copy(wv, wbuf.at[:, pl.ds(HEAD_DIM, HEAD_DIM)], local_sem.at[1]),
        pltpu.make_async_copy(wq, wbuf.at[:, pl.ds(2 * HEAD_DIM, 1024)], local_sem.at[2]),
        pltpu.make_async_copy(keys, kbuf, local_sem.at[3]),
        pltpu.make_async_copy(values, vbuf, local_sem.at[4]),
    ]
    for load in loads:
        load.start()

    barrier = pltpu.get_barrier_semaphore()
    for i in range(8):
        for o in range(8):
            if (i, o) != (0, 0):
                pl.semaphore_signal(
                    barrier, inc=1, device_id=(lax.rem(g + i, 8), r, lax.rem(c + o, 8)), device_id_type=MESH
                )
    for i in range(1, 8):
        pl.semaphore_signal(barrier, inc=1, device_id=(g, lax.rem(r + i, 8), c), device_id_type=MESH)

    def fill(target_group):
        for k in range(CAP):
            j = idx[0, SEND + target_group * CAP + k]
            row = rows[j]
            for cc in range(8):
                outg[target_group * 8 + cc, k] = row[:, cc * 128 : (cc + 1) * 128]

    order = (4, 3, 5, 2, 6, 1, 7, 0)
    fill(lax.rem(g + order[0], 8))
    pl.semaphore_wait(barrier, 70)

    for n, i in enumerate(order):
        tg = lax.rem(g + i, 8)
        if n:
            fill(tg)
        for o in range(8):
            tc = lax.rem(c + o, 8)
            if (i, o) == (0, 0):
                arrv[me] = outg[me]
                continue
            pltpu.make_async_remote_copy(
                src_ref=outg.at[tg * 8 + tc],
                dst_ref=arrv.at[me],
                send_sem=d_send,
                recv_sem=d_recv,
                device_id=(tg, r, tc),
                device_id_type=MESH,
            ).start()
    whole_wait(arrv.at[pl.ds(0, 63)], d_recv)

    x, p = lax.div(c, 2), lax.rem(c, 2)
    ahead = lax.rem(x + 1 + 2 * p, 4) * 2 + p
    behind = lax.rem(x + 3 + 2 * p, 4) * 2 + p
    far = lax.rem(x + 2, 4) * 2 + p
    sibling = c + 1 - 2 * p
    block_of = [lax.rem(r + o + 8, 8) for o in OFFSETS]

    def ag_copy(t, origin, target, kind):
        k = block_of[t]
        return pltpu.make_async_remote_copy(
            src_ref=xg.at[k, origin],
            dst_ref=xg.at[k, origin],
            send_sem=ag_send,
            recv_sem=ag_recv.at[t, kind],
            device_id=(g, r, target),
            device_id_type=MESH,
        )

    def ag_wait(t, kind):
        whole_wait(xg.at[block_of[t], c], ag_recv.at[t, kind])

    def ag_start(t):
        k = block_of[t]
        for a in range(12):
            xg[k, c, a] = arrv[lax.div(idx[0, RECV + k * 12 + a], CAP), lax.rem(idx[0, RECV + k * 12 + a], CAP)]
        ag_copy(t, c, ahead, 1).start()
        ag_copy(t, c, behind, 2).start()
        ag_copy(t, c, sibling, 0).start()

    def ag_first(t):
        ag_wait(t, 1)
        ag_copy(t, behind, ahead, 3).start()
        ag_copy(t, behind, sibling, 4).start()
        ag_wait(t, 2)
        ag_copy(t, ahead, sibling, 5).start()

    def ag_second(t):
        ag_wait(t, 3)
        ag_copy(t, far, sibling, 6).start()

    def ag_finish(t):
        for kind in (0, 4, 5, 6):
            ag_wait(t, kind)

    def tokens(t):
        k = block_of[t]
        return jnp.concatenate([xg[k, cc].reshape(12 * SLOTS, 128) for cc in range(8)], axis=1)

    up, down = lax.rem(r + 1, 8), lax.rem(r + 7, 8)
    toward = (up, down)

    def columns(gi, half):
        first, width = COLUMNS[gi]
        return pl.ds(first + half * width, width)

    def partial(gi, half, t):
        return jnp.dot(tokens(t), wbuf[:, columns(gi, half)], preferred_element_type=jnp.float32)

    def rs_wait(gi, direction, m):
        whole_wait(rbuf[gi][direction].at[m], rs_recv.at[gi, direction, m])

    def rs_step(gi, m):
        is_long, distance = MESSAGES[m]
        for direction in (PLUS, MINUS):
            half = direction if is_long else 1 - direction
            t = OFFSETS.index(distance if direction == PLUS or distance == 4 else -distance)
            part = partial(gi, half, t)
            if (is_long, distance + 1) in MESSAGES:
                before = MESSAGES.index((is_long, distance + 1))
                rs_wait(gi, direction, before)
                part = part + rbuf[gi][direction][before].astype(jnp.float32)
            sbuf[gi][direction][m] = part.astype(jnp.bfloat16)
            pltpu.make_async_remote_copy(
                src_ref=sbuf[gi][direction].at[m],
                dst_ref=rbuf[gi][direction].at[m],
                send_sem=rs_send.at[gi, direction],
                recv_sem=rs_recv.at[gi, direction, m],
                device_id=(g, toward[direction], c),
                device_id_type=MESH,
            ).start()

    def rotate(u):
        return u * cosine[...] + pltpu.roll(u, 64, 1) * sine[...]

    def finish(gi):
        start = 0
        for half in (0, 1):
            own = partial(gi, half, 7)
            for direction in (PLUS, MINUS):
                m = message_index(direction, half, 1)
                rs_wait(gi, direction, m)
                own = own + rbuf[gi][direction][m].astype(jnp.float32)
            for b in range(COLUMNS[gi][1] // 128):
                piece = own[:, b * 128 : (b + 1) * 128]
                at = start + b - (2 if gi == 0 else 0)
                if at == -2:
                    kn[...] = rotate(piece).astype(jnp.bfloat16).reshape(12, SLOTS, 128)
                elif at == -1:
                    vn[...] = piece.astype(jnp.bfloat16).reshape(12, SLOTS, 128)
                else:
                    qs[gi][:, at] = rotate(piece).astype(jnp.bfloat16).reshape(12, SLOTS, 128)
            start += COLUMNS[gi][1] // 128

    def attend(gi):
        heads = GROUPS[gi]
        n = heads * SLOTS
        scale = HEAD_DIM ** (-0.5) * float(np.log2(np.e))
        row_s = lax.broadcasted_iota(jnp.int32, (n, SLOTS), 0) % SLOTS
        col_t = lax.broadcasted_iota(jnp.int32, (n, SLOTS), 1)
        causal = col_t <= row_s
        place = lax.broadcasted_iota(jnp.int32, (n, 512), 1)
        slot = lax.broadcasted_iota(jnp.int32, (n, 128), 0) % SLOTS
        i = lax.broadcasted_iota(jnp.int32, (n, n), 0)
        j = lax.broadcasted_iota(jnp.int32, (n, n), 1)
        swap = ((i % heads) * SLOTS + i // heads == j).astype(jnp.float32).astype(jnp.bfloat16)
        last = (((1,), (1,)), ((), ()))

        def one(a, _):
            length, count = idx[0, LENS + a], idx[0, CNTS + a]
            q = qs[gi][a].reshape(n, 128)
            s1 = lax.dot_general(q, kbuf[a], last, preferred_element_type=jnp.float32) * scale
            s2 = lax.dot_general(q, kn[a], last, preferred_element_type=jnp.float32) * scale
            s1 = jnp.where(place < length, s1, floor_score)
            s2 = jnp.where(causal & (col_t < count), s2, floor_score)
            top = jnp.maximum(jnp.max(s1, axis=1, keepdims=True), jnp.max(s2, axis=1, keepdims=True))
            p1, p2 = jnp.exp2(s1 - top), jnp.exp2(s2 - top)
            den = jnp.sum(p1, axis=1, keepdims=True) + jnp.sum(p2, axis=1, keepdims=True)
            mixed = jnp.dot(p1.astype(jnp.bfloat16), vbuf[a], preferred_element_type=jnp.float32)
            mixed = mixed + jnp.dot(p2.astype(jnp.bfloat16), vn[a], preferred_element_type=jnp.float32)
            mixed = jnp.where(slot < count, mixed / den, 0.0).astype(jnp.bfloat16)
            swapped = jnp.dot(swap, mixed, preferred_element_type=jnp.float32).astype(jnp.bfloat16)
            zs[gi][:, a] = swapped.reshape(8, 2 * heads, 128)
            return 0

        lax.fori_loop(0, 12, one, 0, unroll=2)

    def z_start(gi):
        for i in (4, 3, 5, 2, 6, 1, 7):
            other = lax.rem(r + i, 8)
            pltpu.make_async_remote_copy(
                src_ref=zs[gi].at[other],
                dst_ref=zr[gi].at[r],
                send_sem=z_send.at[gi],
                recv_sem=z_recv.at[gi],
                device_id=(g, other, c),
                device_id_type=MESH,
            ).start()
        zr[gi][r] = zs[gi][r]

    def back_start(gi):
        whole_wait(zr[gi].at[pl.ds(0, 7)], z_recv.at[gi])
        for i in order:
            tg = lax.rem(g + i, 8)
            for o in range(8):
                tc = lax.rem(c + o, 8)
                target = tg * 8 + tc
                for k in range(CAP):
                    a = idx[0, BACK + target * CAP + k]
                    bo[gi][target, k] = zr[gi][lax.div(a, 12), lax.rem(a, 12)]
                if (i, o) == (0, 0):
                    inc[gi][g, c] = bo[gi][target]
                    continue
                pltpu.make_async_remote_copy(
                    src_ref=bo[gi].at[target],
                    dst_ref=inc[gi].at[g, c],
                    send_sem=b_send.at[gi],
                    recv_sem=b_recv.at[gi],
                    device_id=(tg, r, tc),
                    device_id_type=MESH,
                ).start()

    def back_finish(gi):
        whole_wait(bo[gi].at[pl.ds(0, 63)], b_recv.at[gi])
        for j in range(12):
            out[j, :, gi] = inc[gi][idx[0, FING + j], :, idx[0, FINK + j]]

    for t in (0, 1, 2):
        ag_start(t)
    ag_first(0)
    for t in (3, 4):
        ag_start(t)
    ag_second(0)
    ag_first(1)
    ag_first(2)
    for t in (5, 6, 7):
        ag_start(t)
    for load in loads[:3]:
        load.wait()
    ag_finish(0)
    rs_step(0, 0)
    for t in (1, 2):
        ag_second(t)
    for t in (3, 4):
        ag_first(t)
    for t in (1, 2):
        ag_finish(t)
    rs_step(0, 1)
    for t in (3, 4):
        ag_second(t)
    for t in (5, 6, 7):
        ag_first(t)
    rs_step(0, 2)
    for t in (5, 6, 7):
        ag_second(t)
    for t in (3, 4):
        ag_finish(t)
    rs_step(0, 3)
    for t in (5, 6, 7):
        ag_finish(t)
    for m in (4, 5, 6):
        rs_step(0, m)
    for load in loads[3:]:
        load.wait()

    if N_GROUPS == 1:
        finish(0)
        attend(0)
        z_start(0)
        back_start(0)
        back_finish(0)
    else:
        rs_step(1, 0)
        rs_step(1, 1)
        finish(0)
        rs_step(1, 2)
        attend(0)
        z_start(0)
        rs_step(1, 3)
        rs_step(1, 4)
        back_start(0)
        rs_step(1, 5)
        rs_step(1, 6)
        finish(1)
        attend(1)
        z_start(1)
        back_finish(0)
        back_start(1)
        back_finish(1)

    whole_wait(outg.at[pl.ds(0, 63)], d_send)
    whole_wait(xg.at[pl.ds(0, 7)], ag_send)
    for gi in range(N_GROUPS):
        for direction in (PLUS, MINUS):
            whole_wait(sbuf[gi][direction], rs_send.at[gi, direction])
        whole_wait(zs[gi].at[pl.ds(0, 7)], z_send.at[gi])
        whole_wait(bo[gi].at[pl.ds(0, 63)], b_send.at[gi])


def local(
    new_rows,
    query_weight,
    key_weight,
    value_weight,
    cache_keys,
    cache_values,
    region_agents,
    new_counts,
    cache_lengths,
):
    g = lax.axis_index("grp")
    r = lax.axis_index("row")
    c = lax.axis_index("col")
    per_group = 96
    ra = region_agents.reshape(64, 12)
    earlier = jnp.arange(12)[:, None] > jnp.arange(12)[None, :]
    three = jnp.arange(CAP, dtype=jnp.int32)
    mine = lax.dynamic_slice_in_dim(region_agents, (g * 8 + c) * 12, 12) // per_group
    mine_bucket = jnp.sum(((mine[:, None] == mine[None, :]) & earlier).astype(jnp.int32), axis=1)
    pick = (mine[:, None, None] == jnp.arange(8, dtype=jnp.int32)[None, :, None]) & (
        mine_bucket[:, None, None] == three[None, None, :]
    )
    send = jnp.sum(jnp.where(pick, jnp.arange(12, dtype=jnp.int32)[:, None, None], 0), axis=0).reshape(24)
    here = ra // per_group == g
    bucket = jnp.sum((here[:, None, :] & earlier[None]).astype(jnp.int32), axis=2)
    number = jnp.where(here, ra - g * per_group, -1)
    back = jnp.sum(
        jnp.where(here[:, :, None] & (bucket[:, :, None] == three[None, None, :]), number[:, :, None], 0), axis=1
    ).reshape(192)
    place = jnp.arange(64, dtype=jnp.int32)[:, None] * CAP + bucket
    recv = jnp.sum(
        jnp.where(
            number.reshape(1, 768) == jnp.arange(per_group, dtype=jnp.int32)[:, None], place.reshape(1, 768), 0
        ),
        axis=1,
    )
    first = g * per_group + r * 12
    lengths = lax.dynamic_slice_in_dim(cache_lengths, first, 12)
    counts = lax.dynamic_slice_in_dim(new_counts, first, 12)
    table = jnp.concatenate([send, recv, back, mine, mine_bucket, lengths, counts]).reshape(1, 360)

    positions = (lengths[:, None] + jnp.arange(SLOTS, dtype=jnp.int32)[None, :]).astype(jnp.float32)
    exponent = jnp.arange(64, dtype=jnp.float32) * (2.0 / HEAD_DIM)
    angles = positions.reshape(192, 1) * (rotary_base ** (-exponent))
    cosine, sine = jnp.cos(angles), jnp.sin(angles)
    cosine = jnp.concatenate([cosine, cosine], axis=1)
    sine = jnp.concatenate([-sine, sine], axis=1)

    bf, vmem = jnp.bfloat16, pltpu.VMEM
    scratch = [
        vmem((64, CAP, SLOTS, 128), bf),
        vmem((64, CAP, SLOTS, 128), bf),
        vmem((8, 8, 12, SLOTS, 128), bf),
        vmem((1024, 1280), bf),
        vmem((12, 512, 128), bf),
        vmem((12, 512, 128), bf),
        vmem((12, SLOTS, 128), bf),
        vmem((12, SLOTS, 128), bf),
    ]
    for _ in range(2):
        for gi in range(N_GROUPS):
            scratch += [vmem((7, 192, COLUMNS[gi][1]), bf)] * 2
    scratch += [vmem((12, h, SLOTS, 128), bf) for h in GROUPS]
    scratch += [vmem((8, 12, 2 * h, 128), bf) for h in GROUPS] * 2
    scratch += [vmem((64, CAP, 2 * h, 128), bf) for h in GROUPS]
    scratch += [vmem((8, 8, CAP, 2 * h, 128), bf) for h in GROUPS]
    dma = pltpu.SemaphoreType.DMA
    scratch += [
        dma((5,)),
        dma(()),
        dma(()),
        dma(()),
        dma((8, 7)),
        dma((N_GROUPS, 2)),
        dma((N_GROUPS, 2, 7)),
        dma((N_GROUPS,)),
        dma((N_GROUPS,)),
        dma((N_GROUPS,)),
        dma((N_GROUPS,)),
    ]
    in_vmem = pl.BlockSpec(memory_space=pltpu.VMEM)
    anywhere = pl.BlockSpec(memory_space=pl.ANY)
    heads = GROUPS[0]
    result = pl.pallas_call(
        kernel,
        out_shape=jax.ShapeDtypeStruct((12, 8, N_GROUPS, 2 * heads, 128), bf),
        in_specs=[pl.BlockSpec(memory_space=pltpu.SMEM)] + [in_vmem] * 3 + [anywhere] * 5,
        out_specs=in_vmem,
        scratch_shapes=scratch,
        compiler_params=pltpu.CompilerParams(
            collective_id=0, has_side_effects=True, vmem_limit_bytes=56 * 2**20
        ),
    )(table, cosine, sine, new_rows, query_weight, key_weight, value_weight, cache_keys, cache_values)
    return (
        result.reshape(12, 8, N_GROUPS, 2, heads, 128).transpose(0, 3, 1, 2, 4, 5).reshape(12, 2, 8192)
    )


def solution(mesh):
    placed = (
        P(("grp", "col"), None, "row"),
        P("row", "col"),
        P("row", "col"),
        P("row", "col"),
        P(("grp", "row"), None, "col"),
        P(("grp", "row"), None, "col"),
        P(),
        P(),
        P(),
    )
    return jax.shard_map(
        local, mesh=mesh, in_specs=placed, out_specs=P(("grp", "col"), "row", None), check_vma=False
    )
```

```python
import jax
import jax.numpy as jnp
import numpy as np
from jax import lax
from jax.experimental import pallas as pl
from jax.experimental.pallas import tpu as pltpu
from jax.sharding import PartitionSpec as P

HEAD_DIM = 128
SLOTS = 16
CAP = 3
rotary_base = 500000.0
floor_score = -1e30
MESH = pl.DeviceIdType.MESH
SEND, RECV, BACK, SEAT, LENS, CNTS, TABLE = 0, 24, 120, 312, 328, 344, 360

GROUPS = (4, 4)
N_GROUPS = len(GROUPS)
N_ROW = 8
PLUS, MINUS = 0, 1
MESSAGES = ((1, 4), (0, 3), (1, 3), (0, 2), (1, 2), (0, 1), (1, 1))
OFFSETS = (4, 3, -3, 2, -2, 1, -1, 0)


def group_columns():
    found, at = [], 0
    for i, heads in enumerate(GROUPS):
        width = (heads + (2 if i == 0 else 0)) * HEAD_DIM
        found.append((at, width // 2))
        at += width
    return found


COLUMNS = group_columns()


def message_index(direction, half, distance):
    long = 1 if half == direction else 0
    return MESSAGES.index((long, distance))


def whole_wait(ref, sem):
    pltpu.make_async_copy(ref, ref, sem).wait()


def kernel(*refs):
    refs = list(refs)
    take = lambda n: [refs.pop(0) for _ in range(n)]
    agents, all_counts, all_lengths, frequency, rows, wq, wk, wv, keys, values = take(10)
    (out,) = take(1)
    table, idx, cosine, sine = take(4)
    outg, arrv, xg, wbuf, kbuf, vbuf, kn, vn = take(8)
    sbuf = [take(2) for _ in range(N_GROUPS)]
    rbuf = [take(2) for _ in range(N_GROUPS)]
    qs, zs, zr, bo, inc = (take(N_GROUPS) for _ in range(5))
    local_sem, d_send, d_recv, ag_send, ag_recv, rs_send, rs_recv, z_send, z_recv, b_send, b_recv = take(11)

    g = lax.axis_index("grp")
    r = lax.axis_index("row")
    c = lax.axis_index("col")
    me = g * 8 + c

    loads = [
        pltpu.make_async_copy(wk, wbuf.at[:, pl.ds(0, HEAD_DIM)], local_sem.at[0]),
        pltpu.make_async_copy(wv, wbuf.at[:, pl.ds(HEAD_DIM, HEAD_DIM)], local_sem.at[1]),
        pltpu.make_async_copy(wq, wbuf.at[:, pl.ds(2 * HEAD_DIM, 1024)], local_sem.at[2]),
        pltpu.make_async_copy(keys, kbuf, local_sem.at[3]),
        pltpu.make_async_copy(values, vbuf, local_sem.at[4]),
    ]
    for load in loads:
        load.start()

    barrier = pltpu.get_barrier_semaphore()
    for i in range(8):
        for o in range(8):
            if (i, o) != (0, 0):
                pl.semaphore_signal(
                    barrier, inc=1, device_id=(lax.rem(g + i, 8), r, lax.rem(c + o, 8)), device_id_type=MESH
                )
    for i in range(1, 8):
        pl.semaphore_signal(barrier, inc=1, device_id=(g, lax.rem(r + i, 8), c), device_id_type=MESH)

    ra = agents[...]
    flat = lax.broadcasted_iota(jnp.int32, (1, 768), 1)
    region = lax.shift_right_logical(flat * 5462, 16)
    within = flat - region * 12
    served = lax.shift_right_logical(ra * 683, 16)
    bucket = jnp.zeros((1, 768), jnp.int32)
    for d in range(1, 12):
        same = (pltpu.roll(served, d, 1) == served) & (within >= d)
        bucket = bucket + same.astype(jnp.int32)
    place = region * CAP + bucket
    seat = served * CAP + bucket

    def pick(count, chosen, offset, values, most):
        want = lax.broadcasted_iota(jnp.int32, (count, 768), 0) + offset
        hit = jnp.broadcast_to(chosen, (count, 768)) == want
        total = jnp.sum(jnp.where(hit, jnp.broadcast_to(values, (count, 768)), 0), axis=1, keepdims=True)
        return jnp.broadcast_to(jnp.clip(total, 0, most), (count, 128))

    table[SEND : SEND + 24] = pick(24, jnp.where(region == me, seat, -1), 0, within, 11)
    table[RECV : RECV + 96] = pick(96, ra, g * 96, place, 64 * CAP - 1)
    table[BACK : BACK + 192] = pick(192, jnp.where(served == g, place, -1), 0, ra - g * 96, 95)
    table[SEAT : SEAT + 16] = pick(16, flat, me * 12, seat, 8 * CAP - 1)
    table[LENS : LENS + 16] = pick(16, flat, g * 96 + r * 12, all_lengths[...], 512)
    table[CNTS : CNTS + 16] = pick(16, flat, g * 96 + r * 12, all_counts[...], SLOTS)
    to_scalars = pltpu.make_async_copy(table, idx, local_sem.at[5])
    to_scalars.start()
    to_scalars.wait()

    def fill(target_group):
        for k in range(CAP):
            j = idx[SEND + target_group * CAP + k, 0]
            row = rows[j]
            for cc in range(8):
                outg[target_group * 8 + cc, k] = row[:, cc * 128 : (cc + 1) * 128]

    order = (4, 3, 5, 2, 6, 1, 7, 0)
    fill(lax.rem(g + order[0], 8))
    pl.semaphore_wait(barrier, 70)

    for n, i in enumerate(order):
        tg = lax.rem(g + i, 8)
        if n:
            fill(tg)
        for o in range(8):
            tc = lax.rem(c + o, 8)
            if (i, o) == (0, 0):
                arrv[me] = outg[me]
                continue
            pltpu.make_async_remote_copy(
                src_ref=outg.at[tg * 8 + tc],
                dst_ref=arrv.at[me],
                send_sem=d_send,
                recv_sem=d_recv,
                device_id=(tg, r, tc),
                device_id_type=MESH,
            ).start()

    slots = lax.broadcasted_iota(jnp.int32, (SLOTS, 128), 0)
    lanes = lax.broadcasted_iota(jnp.int32, (SLOTS, 128), 1)
    for a in range(12):
        angle = (slots + idx[LENS + a, 0]).astype(jnp.float32) * frequency[...]
        cosine[a * SLOTS : (a + 1) * SLOTS] = jnp.cos(angle)
        turn = jnp.sin(angle)
        sine[a * SLOTS : (a + 1) * SLOTS] = jnp.where(lanes < 64, -turn, turn)
    whole_wait(arrv.at[pl.ds(0, 63)], d_recv)

    x, p = lax.div(c, 2), lax.rem(c, 2)
    ahead = lax.rem(x + 1 + 2 * p, 4) * 2 + p
    behind = lax.rem(x + 3 + 2 * p, 4) * 2 + p
    far = lax.rem(x + 2, 4) * 2 + p
    sibling = c + 1 - 2 * p
    block_of = [lax.rem(r + o + 8, 8) for o in OFFSETS]

    def ag_copy(t, origin, target, kind):
        k = block_of[t]
        return pltpu.make_async_remote_copy(
            src_ref=xg.at[k, origin],
            dst_ref=xg.at[k, origin],
            send_sem=ag_send,
            recv_sem=ag_recv.at[t, kind],
            device_id=(g, r, target),
            device_id_type=MESH,
        )

    def ag_wait(t, kind):
        whole_wait(xg.at[block_of[t], c], ag_recv.at[t, kind])

    def ag_start(t):
        k = block_of[t]
        for a in range(12):
            xg[k, c, a] = arrv[lax.div(idx[RECV + k * 12 + a, 0], CAP), lax.rem(idx[RECV + k * 12 + a, 0], CAP)]
        ag_copy(t, c, ahead, 1).start()
        ag_copy(t, c, behind, 2).start()
        ag_copy(t, c, sibling, 0).start()

    def ag_first(t):
        ag_wait(t, 1)
        ag_copy(t, behind, ahead, 3).start()
        ag_copy(t, behind, sibling, 4).start()
        ag_wait(t, 2)
        ag_copy(t, ahead, sibling, 5).start()

    def ag_second(t):
        ag_wait(t, 3)
        ag_copy(t, far, sibling, 6).start()

    def ag_finish(t):
        for kind in (0, 4, 5, 6):
            ag_wait(t, kind)

    def tokens(t):
        k = block_of[t]
        return jnp.concatenate([xg[k, cc].reshape(12 * SLOTS, 128) for cc in range(8)], axis=1)

    up, down = lax.rem(r + 1, 8), lax.rem(r + 7, 8)
    toward = (up, down)

    def columns(gi, half):
        first, width = COLUMNS[gi]
        return pl.ds(first + half * width, width)

    def partial(gi, half, t):
        return jnp.dot(tokens(t), wbuf[:, columns(gi, half)], preferred_element_type=jnp.float32)

    def rs_wait(gi, direction, m):
        whole_wait(rbuf[gi][direction].at[m], rs_recv.at[gi, direction, m])

    def rs_step(gi, m):
        is_long, distance = MESSAGES[m]
        for direction in (PLUS, MINUS):
            half = direction if is_long else 1 - direction
            t = OFFSETS.index(distance if direction == PLUS or distance == 4 else -distance)
            part = partial(gi, half, t)
            if (is_long, distance + 1) in MESSAGES:
                before = MESSAGES.index((is_long, distance + 1))
                rs_wait(gi, direction, before)
                part = part + rbuf[gi][direction][before].astype(jnp.float32)
            sbuf[gi][direction][m] = part.astype(jnp.bfloat16)
            pltpu.make_async_remote_copy(
                src_ref=sbuf[gi][direction].at[m],
                dst_ref=rbuf[gi][direction].at[m],
                send_sem=rs_send.at[gi, direction],
                recv_sem=rs_recv.at[gi, direction, m],
                device_id=(g, toward[direction], c),
                device_id_type=MESH,
            ).start()

    def rotate(u):
        return u * cosine[...] + pltpu.roll(u, 64, 1) * sine[...]

    def finish(gi):
        start = 0
        for half in (0, 1):
            own = partial(gi, half, 7)
            for direction in (PLUS, MINUS):
                m = message_index(direction, half, 1)
                rs_wait(gi, direction, m)
                own = own + rbuf[gi][direction][m].astype(jnp.float32)
            for b in range(COLUMNS[gi][1] // 128):
                piece = own[:, b * 128 : (b + 1) * 128]
                at = start + b - (2 if gi == 0 else 0)
                if at == -2:
                    kn[...] = rotate(piece).astype(jnp.bfloat16).reshape(12, SLOTS, 128)
                elif at == -1:
                    vn[...] = piece.astype(jnp.bfloat16).reshape(12, SLOTS, 128)
                else:
                    qs[gi][:, at] = rotate(piece).astype(jnp.bfloat16).reshape(12, SLOTS, 128)
            start += COLUMNS[gi][1] // 128

    def attend(gi):
        heads = GROUPS[gi]
        n = heads * SLOTS
        scale = HEAD_DIM ** (-0.5) * float(np.log2(np.e))
        row_s = lax.broadcasted_iota(jnp.int32, (n, SLOTS), 0) % SLOTS
        col_t = lax.broadcasted_iota(jnp.int32, (n, SLOTS), 1)
        causal = col_t <= row_s
        place = lax.broadcasted_iota(jnp.int32, (n, 512), 1)
        slot = lax.broadcasted_iota(jnp.int32, (n, 128), 0) % SLOTS
        i = lax.broadcasted_iota(jnp.int32, (n, n), 0)
        j = lax.broadcasted_iota(jnp.int32, (n, n), 1)
        swap = ((i % heads) * SLOTS + i // heads == j).astype(jnp.float32).astype(jnp.bfloat16)
        last = (((1,), (1,)), ((), ()))

        def one(a, _):
            length, count = idx[LENS + a, 0], idx[CNTS + a, 0]
            q = qs[gi][a].reshape(n, 128)
            s1 = lax.dot_general(q, kbuf[a], last, preferred_element_type=jnp.float32) * scale
            s2 = lax.dot_general(q, kn[a], last, preferred_element_type=jnp.float32) * scale
            s1 = jnp.where(place < length, s1, floor_score)
            s2 = jnp.where(causal & (col_t < count), s2, floor_score)
            top = jnp.maximum(jnp.max(s1, axis=1, keepdims=True), jnp.max(s2, axis=1, keepdims=True))
            p1, p2 = jnp.exp2(s1 - top), jnp.exp2(s2 - top)
            den = jnp.sum(p1, axis=1, keepdims=True) + jnp.sum(p2, axis=1, keepdims=True)
            mixed = jnp.dot(p1.astype(jnp.bfloat16), vbuf[a], preferred_element_type=jnp.float32)
            mixed = mixed + jnp.dot(p2.astype(jnp.bfloat16), vn[a], preferred_element_type=jnp.float32)
            mixed = jnp.where(slot < count, mixed / den, 0.0).astype(jnp.bfloat16)
            swapped = jnp.dot(swap, mixed, preferred_element_type=jnp.float32).astype(jnp.bfloat16)
            zs[gi][:, a] = swapped.reshape(8, 2 * heads, 128)
            return 0

        lax.fori_loop(0, 12, one, 0, unroll=2)

    def z_start(gi):
        for i in (4, 3, 5, 2, 6, 1, 7):
            other = lax.rem(r + i, 8)
            pltpu.make_async_remote_copy(
                src_ref=zs[gi].at[other],
                dst_ref=zr[gi].at[r],
                send_sem=z_send.at[gi],
                recv_sem=z_recv.at[gi],
                device_id=(g, other, c),
                device_id_type=MESH,
            ).start()
        zr[gi][r] = zs[gi][r]

    def back_start(gi):
        whole_wait(zr[gi].at[pl.ds(0, 7)], z_recv.at[gi])
        for i in order:
            tg = lax.rem(g + i, 8)
            for o in range(8):
                tc = lax.rem(c + o, 8)
                target = tg * 8 + tc
                for k in range(CAP):
                    a = idx[BACK + target * CAP + k, 0]
                    bo[gi][target, k] = zr[gi][lax.div(a, 12), lax.rem(a, 12)]
                if (i, o) == (0, 0):
                    inc[gi][g, c] = bo[gi][target]
                    continue
                pltpu.make_async_remote_copy(
                    src_ref=bo[gi].at[target],
                    dst_ref=inc[gi].at[g, c],
                    send_sem=b_send.at[gi],
                    recv_sem=b_recv.at[gi],
                    device_id=(tg, r, tc),
                    device_id_type=MESH,
                ).start()

    def back_finish(gi):
        whole_wait(bo[gi].at[pl.ds(0, 63)], b_recv.at[gi])
        for j in range(12):
            seat_j = idx[SEAT + j, 0]
            out[j, :, gi] = inc[gi][lax.div(seat_j, CAP), :, lax.rem(seat_j, CAP)]

    for t in (0, 1, 2):
        ag_start(t)
    ag_first(0)
    for t in (3, 4):
        ag_start(t)
    ag_second(0)
    ag_first(1)
    ag_first(2)
    for t in (5, 6, 7):
        ag_start(t)
    for load in loads[:3]:
        load.wait()
    ag_finish(0)
    rs_step(0, 0)
    for t in (1, 2):
        ag_second(t)
    for t in (3, 4):
        ag_first(t)
    for t in (1, 2):
        ag_finish(t)
    rs_step(0, 1)
    for t in (3, 4):
        ag_second(t)
    for t in (5, 6, 7):
        ag_first(t)
    rs_step(0, 2)
    for t in (5, 6, 7):
        ag_second(t)
    for t in (3, 4):
        ag_finish(t)
    rs_step(0, 3)
    for t in (5, 6, 7):
        ag_finish(t)
    for m in (4, 5, 6):
        rs_step(0, m)
    for load in loads[3:]:
        load.wait()

    if N_GROUPS == 1:
        finish(0)
        attend(0)
        z_start(0)
        back_start(0)
        back_finish(0)
    else:
        rs_step(1, 0)
        rs_step(1, 1)
        finish(0)
        rs_step(1, 2)
        attend(0)
        z_start(0)
        rs_step(1, 3)
        rs_step(1, 4)
        back_start(0)
        rs_step(1, 5)
        rs_step(1, 6)
        finish(1)
        attend(1)
        z_start(1)
        back_finish(0)
        back_start(1)
        back_finish(1)

    whole_wait(outg.at[pl.ds(0, 63)], d_send)
    whole_wait(xg.at[pl.ds(0, 7)], ag_send)
    for gi in range(N_GROUPS):
        for direction in (PLUS, MINUS):
            whole_wait(sbuf[gi][direction], rs_send.at[gi, direction])
        whole_wait(zs[gi].at[pl.ds(0, 7)], z_send.at[gi])
        whole_wait(bo[gi].at[pl.ds(0, 63)], b_send.at[gi])


def local(
    new_rows,
    query_weight,
    key_weight,
    value_weight,
    cache_keys,
    cache_values,
    region_agents,
    new_counts,
    cache_lengths,
):
    half_frequency = rotary_base ** (-np.arange(64) * (2.0 / HEAD_DIM))
    frequency = jnp.asarray(np.tile(half_frequency, 2).astype(np.float32).reshape(1, 128))
    bf, vmem = jnp.bfloat16, pltpu.VMEM
    scratch = [
        vmem((TABLE, 128), jnp.int32),
        pltpu.SMEM((TABLE, 128), jnp.int32),
        vmem((192, 128), jnp.float32),
        vmem((192, 128), jnp.float32),
        vmem((64, CAP, SLOTS, 128), bf),
        vmem((64, CAP, SLOTS, 128), bf),
        vmem((8, 8, 12, SLOTS, 128), bf),
        vmem((1024, 1280), bf),
        vmem((12, 512, 128), bf),
        vmem((12, 512, 128), bf),
        vmem((12, SLOTS, 128), bf),
        vmem((12, SLOTS, 128), bf),
    ]
    for _ in range(2):
        for gi in range(N_GROUPS):
            scratch += [vmem((7, 192, COLUMNS[gi][1]), bf)] * 2
    scratch += [vmem((12, h, SLOTS, 128), bf) for h in GROUPS]
    scratch += [vmem((8, 12, 2 * h, 128), bf) for h in GROUPS] * 2
    scratch += [vmem((64, CAP, 2 * h, 128), bf) for h in GROUPS]
    scratch += [vmem((8, 8, CAP, 2 * h, 128), bf) for h in GROUPS]
    dma = pltpu.SemaphoreType.DMA
    scratch += [
        dma((6,)),
        dma(()),
        dma(()),
        dma(()),
        dma((8, 7)),
        dma((N_GROUPS, 2)),
        dma((N_GROUPS, 2, 7)),
        dma((N_GROUPS,)),
        dma((N_GROUPS,)),
        dma((N_GROUPS,)),
        dma((N_GROUPS,)),
    ]
    in_vmem = pl.BlockSpec(memory_space=pltpu.VMEM)
    anywhere = pl.BlockSpec(memory_space=pl.ANY)
    heads = GROUPS[0]
    result = pl.pallas_call(
        kernel,
        out_shape=jax.ShapeDtypeStruct((12, 8, N_GROUPS, 2 * heads, 128), bf),
        in_specs=[in_vmem] * 5 + [anywhere] * 5,
        out_specs=in_vmem,
        scratch_shapes=scratch,
        compiler_params=pltpu.CompilerParams(
            collective_id=0, has_side_effects=True, vmem_limit_bytes=56 * 2**20
        ),
    )(
        region_agents.reshape(1, 768),
        new_counts.reshape(1, 768),
        cache_lengths.reshape(1, 768),
        frequency,
        new_rows,
        query_weight,
        key_weight,
        value_weight,
        cache_keys,
        cache_values,
    )
    return (
        result.reshape(12, 8, N_GROUPS, 2, heads, 128).transpose(0, 3, 1, 2, 4, 5).reshape(12, 2, 8192)
    )


def solution(mesh):
    placed = (
        P(("grp", "col"), None, "row"),
        P("row", "col"),
        P("row", "col"),
        P("row", "col"),
        P(("grp", "row"), None, "col"),
        P(("grp", "row"), None, "col"),
        P(),
        P(),
        P(),
    )
    return jax.shard_map(
        local, mesh=mesh, in_specs=placed, out_specs=P(("grp", "col"), "row", None), check_vma=False
    )
```

```python
import jax
import jax.numpy as jnp
import numpy as np
from jax import lax
from jax.experimental import pallas as pl
from jax.experimental.pallas import tpu as pltpu
from jax.sharding import PartitionSpec as P

HEAD_DIM = 128
SLOTS = 16
CAP = 3
rotary_base = 500000.0
floor_score = -1e30
MESH = pl.DeviceIdType.MESH
SEND, RECV, BACK, SEAT, LENS, CNTS, TABLE = 0, 24, 120, 312, 328, 344, 360

GROUPS = (4, 4)
N_GROUPS = len(GROUPS)
HALF = SLOTS // 2
TOKENS = 12 * HALF
RUNS = ((0, 0, 1280), (1, 0, 768), (1, 768, 512))
N_RUNS = len(RUNS)
PLUS, MINUS = 0, 1
MESSAGES = ((1, 4), (0, 3), (1, 3), (0, 2), (1, 2), (0, 1), (1, 1))
OFFSETS = (4, 3, -3, 2, -2, 1, -1, 0)


def message_index(direction, half, distance):
    long = 1 if half == direction else 0
    return MESSAGES.index((long, distance))


def whole_wait(ref, sem):
    pltpu.make_async_copy(ref, ref, sem).wait()


def kernel(*refs):
    refs = list(refs)
    take = lambda n: [refs.pop(0) for _ in range(n)]
    agents, some_counts, some_lengths, frequency, rows, wq, wk, wv, keys, values = take(10)
    (out,) = take(1)
    table, idx, cosine, sine = take(4)
    outg, arrv0, arrv1, xg, wbuf, kbuf, vbuf, kn, vn = take(9)
    arrv = (arrv0, arrv1)
    sbuf = [take(2) for _ in range(N_RUNS)]
    rbuf = [take(2) for _ in range(N_RUNS)]
    qs, zs, zr, bo, inc = (take(N_GROUPS) for _ in range(5))
    local_sem, d_send, d_recv, ag_send, ag_recv, rs_send, rs_recv, z_send, z_recv, b_send, b_recv = take(11)

    g = lax.axis_index("grp")
    r = lax.axis_index("row")
    c = lax.axis_index("col")
    me = g * 8 + c

    loads = [
        pltpu.make_async_copy(wk, wbuf.at[:, pl.ds(0, HEAD_DIM)], local_sem.at[0]),
        pltpu.make_async_copy(wv, wbuf.at[:, pl.ds(HEAD_DIM, HEAD_DIM)], local_sem.at[1]),
        pltpu.make_async_copy(wq, wbuf.at[:, pl.ds(2 * HEAD_DIM, 1024)], local_sem.at[2]),
        pltpu.make_async_copy(keys, kbuf, local_sem.at[3]),
        pltpu.make_async_copy(values, vbuf, local_sem.at[4]),
    ]
    for load in loads:
        load.start()

    barrier = pltpu.get_barrier_semaphore()
    for i in range(8):
        for o in range(8):
            if (i, o) != (0, 0):
                pl.semaphore_signal(
                    barrier, inc=1, device_id=(lax.rem(g + i, 8), r, lax.rem(c + o, 8)), device_id_type=MESH
                )
    for i in range(1, 8):
        pl.semaphore_signal(barrier, inc=1, device_id=(g, lax.rem(r + i, 8), c), device_id_type=MESH)

    ra, all_counts, all_lengths = (n[...].reshape(1, 768) for n in (agents, some_counts, some_lengths))
    flat = lax.broadcasted_iota(jnp.int32, (1, 768), 1)
    region = lax.shift_right_logical(flat * 5462, 16)
    within = flat - region * 12
    served = lax.shift_right_logical(ra * 683, 16)
    bucket = jnp.zeros((1, 768), jnp.int32)
    for d in range(1, 12):
        same = (pltpu.roll(served, d, 1) == served) & (within >= d)
        bucket = bucket + same.astype(jnp.int32)
    place = region * CAP + bucket
    seat = served * CAP + bucket

    def pick(count, chosen, offset, values, most):
        want = lax.broadcasted_iota(jnp.int32, (count, 768), 0) + offset
        hit = jnp.broadcast_to(chosen, (count, 768)) == want
        total = jnp.sum(jnp.where(hit, jnp.broadcast_to(values, (count, 768)), 0), axis=1, keepdims=True)
        return jnp.broadcast_to(jnp.clip(total, 0, most), (count, 128))

    table[SEND : SEND + 24] = pick(24, jnp.where(region == me, seat, -1), 0, within, 11)
    table[RECV : RECV + 96] = pick(96, ra, g * 96, place, 64 * CAP - 1)
    table[BACK : BACK + 192] = pick(192, jnp.where(served == g, place, -1), 0, ra - g * 96, 95)
    table[SEAT : SEAT + 16] = pick(16, flat, me * 12, seat, 8 * CAP - 1)
    table[LENS : LENS + 16] = pick(16, flat, g * 96 + r * 12, all_lengths, 512)
    table[CNTS : CNTS + 16] = pick(16, flat, g * 96 + r * 12, all_counts, SLOTS)
    to_scalars = pltpu.make_async_copy(table, idx, local_sem.at[5])
    to_scalars.start()
    to_scalars.wait()

    def fill(s, target_group):
        for k in range(CAP):
            j = idx[SEND + target_group * CAP + k, 0]
            row = rows[j, s]
            for cc in range(8):
                outg[s, target_group * 8 + cc, k] = row[:, cc * 128 : (cc + 1) * 128]

    order = (4, 3, 5, 2, 6, 1, 7, 0)
    fill(0, lax.rem(g + order[0], 8))
    pl.semaphore_wait(barrier, 70)

    def dispatch(s):
        for n, i in enumerate(order):
            tg = lax.rem(g + i, 8)
            if n or s:
                fill(s, tg)
            for o in range(8):
                tc = lax.rem(c + o, 8)
                if (i, o) == (0, 0):
                    arrv[s][me] = outg[s, me]
                    continue
                pltpu.make_async_remote_copy(
                    src_ref=outg.at[s, tg * 8 + tc],
                    dst_ref=arrv[s].at[me],
                    send_sem=d_send.at[s],
                    recv_sem=d_recv.at[s],
                    device_id=(tg, r, tc),
                    device_id_type=MESH,
                ).start()

    def dispatch_wait(s):
        whole_wait(arrv[s].at[pl.ds(0, 63)], d_recv.at[s])

    dispatch(0)
    dispatch(1)

    slots = lax.broadcasted_iota(jnp.int32, (HALF, 128), 0)
    lanes = lax.broadcasted_iota(jnp.int32, (HALF, 128), 1)
    for s in range(2):
        for a in range(12):
            angle = (slots + (idx[LENS + a, 0] + s * HALF)).astype(jnp.float32) * frequency[...]
            cosine[s, a * HALF : (a + 1) * HALF] = jnp.cos(angle)
            turn = jnp.sin(angle)
            sine[s, a * HALF : (a + 1) * HALF] = jnp.where(lanes < 64, -turn, turn)

    x, p = lax.div(c, 2), lax.rem(c, 2)
    ahead = lax.rem(x + 1 + 2 * p, 4) * 2 + p
    behind = lax.rem(x + 3 + 2 * p, 4) * 2 + p
    far = lax.rem(x + 2, 4) * 2 + p
    sibling = c + 1 - 2 * p
    block_of = [lax.rem(r + o + 8, 8) for o in OFFSETS]

    def ag_copy(s, t, origin, target, kind):
        k = block_of[t]
        return pltpu.make_async_remote_copy(
            src_ref=xg.at[s, k, origin],
            dst_ref=xg.at[s, k, origin],
            send_sem=ag_send.at[s],
            recv_sem=ag_recv.at[s, t, kind],
            device_id=(g, r, target),
            device_id_type=MESH,
        )

    def ag_wait(s, t, kind):
        whole_wait(xg.at[s, block_of[t], c], ag_recv.at[s, t, kind])

    def ag_start(s, *ts):
        for t in ts:
            k = block_of[t]
            for a in range(12):
                seat = idx[RECV + k * 12 + a, 0]
                xg[s, k, c, a] = arrv[s][lax.div(seat, CAP), lax.rem(seat, CAP)]
            ag_copy(s, t, c, ahead, 1).start()
            ag_copy(s, t, c, behind, 2).start()
            ag_copy(s, t, c, sibling, 0).start()

    def ag_first(s, *ts):
        for t in ts:
            ag_wait(s, t, 1)
            ag_copy(s, t, behind, ahead, 3).start()
            ag_copy(s, t, behind, sibling, 4).start()
            ag_wait(s, t, 2)
            ag_copy(s, t, ahead, sibling, 5).start()

    def ag_second(s, *ts):
        for t in ts:
            ag_wait(s, t, 3)
            ag_copy(s, t, far, sibling, 6).start()

    def ag_finish(s, *ts):
        for t in ts:
            for kind in (0, 4, 5, 6):
                ag_wait(s, t, kind)

    def tokens(s, t):
        k = block_of[t]
        return jnp.concatenate([xg[s, k, cc].reshape(TOKENS, 128) for cc in range(8)], axis=1)

    up, down = lax.rem(r + 1, 8), lax.rem(r + 7, 8)
    toward = (up, down)

    def partial(run, half, t):
        s, first, width = RUNS[run]
        width = width // 2
        at = pl.ds(first + half * width, width)
        return jnp.dot(tokens(s, t), wbuf[:, at], preferred_element_type=jnp.float32)

    def rs_wait(run, direction, m):
        whole_wait(rbuf[run][direction].at[m], rs_recv.at[run, direction, m])

    def rs_step(run, m):
        is_long, distance = MESSAGES[m]
        for direction in (PLUS, MINUS):
            half = direction if is_long else 1 - direction
            t = OFFSETS.index(distance if direction == PLUS or distance == 4 else -distance)
            part = partial(run, half, t)
            if (is_long, distance + 1) in MESSAGES:
                before = MESSAGES.index((is_long, distance + 1))
                rs_wait(run, direction, before)
                part = part + rbuf[run][direction][before].astype(jnp.float32)
            sbuf[run][direction][m] = part.astype(jnp.bfloat16)
            pltpu.make_async_remote_copy(
                src_ref=sbuf[run][direction].at[m],
                dst_ref=rbuf[run][direction].at[m],
                send_sem=rs_send.at[run, direction],
                recv_sem=rs_recv.at[run, direction, m],
                device_id=(g, toward[direction], c),
                device_id_type=MESH,
            ).start()

    def rotate(u, s):
        return u * cosine[s] + pltpu.roll(u, 64, 1) * sine[s]

    def finish(run):
        s, first, width = RUNS[run]
        blocks = width // 256
        for half in (0, 1):
            own = partial(run, half, 7)
            for direction in (PLUS, MINUS):
                m = message_index(direction, half, 1)
                rs_wait(run, direction, m)
                own = own + rbuf[run][direction][m].astype(jnp.float32)
            for b in range(blocks):
                piece = own[:, b * 128 : (b + 1) * 128]
                head = first // 128 + half * blocks + b - 2
                if head == -2:
                    kn[:, s] = rotate(piece, s).astype(jnp.bfloat16).reshape(12, HALF, 128)
                elif head == -1:
                    vn[:, s] = piece.astype(jnp.bfloat16).reshape(12, HALF, 128)
                else:
                    gi, at = divmod(head, GROUPS[0])
                    qs[gi][:, at, s] = rotate(piece, s).astype(jnp.bfloat16).reshape(12, HALF, 128)

    def attend(gi):
        heads = GROUPS[gi]
        n = heads * SLOTS
        scale = HEAD_DIM ** (-0.5) * float(np.log2(np.e))
        row_s = lax.broadcasted_iota(jnp.int32, (n, SLOTS), 0) % SLOTS
        col_t = lax.broadcasted_iota(jnp.int32, (n, SLOTS), 1)
        causal = col_t <= row_s
        place = lax.broadcasted_iota(jnp.int32, (n, 512), 1)
        slot = lax.broadcasted_iota(jnp.int32, (n, 128), 0) % SLOTS
        i = lax.broadcasted_iota(jnp.int32, (n, n), 0)
        j = lax.broadcasted_iota(jnp.int32, (n, n), 1)
        pair, rest = i // (2 * heads), i % (2 * heads)
        swap = ((rest // 2) * SLOTS + pair * 2 + rest % 2 == j).astype(jnp.float32).astype(jnp.bfloat16)
        last = (((1,), (1,)), ((), ()))

        def one(a, _):
            length, count = idx[LENS + a, 0], idx[CNTS + a, 0]
            q = qs[gi][a].reshape(n, 128)
            s1 = lax.dot_general(q, kbuf[a], last, preferred_element_type=jnp.float32) * scale
            s2 = lax.dot_general(q, kn[a].reshape(SLOTS, 128), last, preferred_element_type=jnp.float32) * scale
            s1 = jnp.where(place < length, s1, floor_score)
            s2 = jnp.where(causal & (col_t < count), s2, floor_score)
            top = jnp.maximum(jnp.max(s1, axis=1, keepdims=True), jnp.max(s2, axis=1, keepdims=True))
            p1, p2 = jnp.exp2(s1 - top), jnp.exp2(s2 - top)
            den = jnp.sum(p1, axis=1, keepdims=True) + jnp.sum(p2, axis=1, keepdims=True)
            mixed = jnp.dot(p1.astype(jnp.bfloat16), vbuf[a], preferred_element_type=jnp.float32)
            mixed = mixed + jnp.dot(p2.astype(jnp.bfloat16), vn[a].reshape(SLOTS, 128), preferred_element_type=jnp.float32)
            mixed = jnp.where(slot < count, mixed / den, 0.0).astype(jnp.bfloat16)
            swapped = jnp.dot(swap, mixed, preferred_element_type=jnp.float32).astype(jnp.bfloat16)
            zs[gi][:, a] = swapped.reshape(8, 2 * heads, 128)
            return 0

        lax.fori_loop(0, 12, one, 0, unroll=2)

    def z_start(gi):
        for i in (4, 3, 5, 2, 6, 1, 7):
            other = lax.rem(r + i, 8)
            pltpu.make_async_remote_copy(
                src_ref=zs[gi].at[other],
                dst_ref=zr[gi].at[r],
                send_sem=z_send.at[gi],
                recv_sem=z_recv.at[gi],
                device_id=(g, other, c),
                device_id_type=MESH,
            ).start()
        zr[gi][r] = zs[gi][r]

    def back_start(gi):
        whole_wait(zr[gi].at[pl.ds(0, 7)], z_recv.at[gi])
        for i in order:
            tg = lax.rem(g + i, 8)
            for o in range(8):
                tc = lax.rem(c + o, 8)
                target = tg * 8 + tc
                for k in range(CAP):
                    a = idx[BACK + target * CAP + k, 0]
                    bo[gi][target, k] = zr[gi][lax.div(a, 12), lax.rem(a, 12)]
                if (i, o) == (0, 0):
                    inc[gi][g, c] = bo[gi][target]
                    continue
                pltpu.make_async_remote_copy(
                    src_ref=bo[gi].at[target],
                    dst_ref=inc[gi].at[g, c],
                    send_sem=b_send.at[gi],
                    recv_sem=b_recv.at[gi],
                    device_id=(tg, r, tc),
                    device_id_type=MESH,
                ).start()

    def back_finish(gi):
        whole_wait(bo[gi].at[pl.ds(0, 63)], b_recv.at[gi])
        for j in range(12):
            seat_j = idx[SEAT + j, 0]
            out[j, :, gi] = inc[gi][lax.div(seat_j, CAP), :, lax.rem(seat_j, CAP)]

    dispatch_wait(0)
    ag_start(0, 0, 1, 2)
    ag_first(0, 0)
    ag_start(0, 3, 4)
    ag_second(0, 0)
    for load in loads[:3]:
        load.wait()
    ag_first(0, 1, 2)
    ag_finish(0, 0)
    rs_step(0, 0)
    ag_start(0, 5, 6, 7)
    ag_second(0, 1, 2)
    ag_first(0, 3, 4)
    ag_finish(0, 1, 2)
    rs_step(0, 1)
    ag_second(0, 3, 4)
    rs_step(0, 2)
    ag_first(0, 5, 6, 7)
    ag_finish(0, 3, 4)
    rs_step(0, 3)
    ag_second(0, 5, 6, 7)
    ag_finish(0, 5, 6, 7)
    dispatch_wait(1)
    ag_start(1, 0, 1, 2, 3, 4)
    rs_step(0, 4)
    ag_first(1, 0, 1, 2)
    ag_start(1, 5, 6, 7)
    rs_step(0, 5)
    ag_second(1, 0, 1, 2)
    ag_first(1, 3, 4)
    rs_step(0, 6)
    ag_finish(1, 0, 1, 2)
    rs_step(1, 0)
    rs_step(1, 1)
    ag_second(1, 3, 4)
    ag_first(1, 5, 6, 7)
    for load in loads[3:]:
        load.wait()
    finish(0)
    rs_step(1, 2)
    ag_second(1, 5, 6, 7)
    ag_finish(1, 3, 4)
    rs_step(1, 3)
    ag_finish(1, 5, 6, 7)
    rs_step(1, 4)
    rs_step(1, 5)
    rs_step(1, 6)
    rs_step(2, 0)
    rs_step(2, 1)
    finish(1)
    rs_step(2, 2)
    attend(0)
    z_start(0)
    rs_step(2, 3)
    rs_step(2, 4)
    back_start(0)
    rs_step(2, 5)
    rs_step(2, 6)
    finish(2)
    attend(1)
    z_start(1)
    back_finish(0)
    back_start(1)
    back_finish(1)

    for s in range(2):
        whole_wait(outg.at[s, pl.ds(0, 63)], d_send.at[s])
        whole_wait(xg.at[s, pl.ds(0, 7)], ag_send.at[s])
    for run in range(N_RUNS):
        for direction in (PLUS, MINUS):
            whole_wait(sbuf[run][direction], rs_send.at[run, direction])
    for gi in range(N_GROUPS):
        whole_wait(zs[gi].at[pl.ds(0, 7)], z_send.at[gi])
        whole_wait(bo[gi].at[pl.ds(0, 63)], b_send.at[gi])


def local(
    new_rows,
    query_weight,
    key_weight,
    value_weight,
    cache_keys,
    cache_values,
    region_agents,
    new_counts,
    cache_lengths,
):
    half_frequency = rotary_base ** (-np.arange(64) * (2.0 / HEAD_DIM))
    frequency = jnp.asarray(np.tile(half_frequency, 2).astype(np.float32).reshape(1, 128))
    bf, vmem = jnp.bfloat16, pltpu.VMEM
    scratch = [
        vmem((TABLE, 128), jnp.int32),
        pltpu.SMEM((TABLE, 128), jnp.int32),
        vmem((2, TOKENS, 128), jnp.float32),
        vmem((2, TOKENS, 128), jnp.float32),
        vmem((2, 64, CAP, HALF, 128), bf),
        vmem((64, CAP, HALF, 128), bf),
        vmem((64, CAP, HALF, 128), bf),
        vmem((2, 8, 8, 12, HALF, 128), bf),
        vmem((1024, 1280), bf),
        vmem((12, 512, 128), bf),
        vmem((12, 512, 128), bf),
        vmem((12, 2, HALF, 128), bf),
        vmem((12, 2, HALF, 128), bf),
    ]
    for _ in range(2):
        for run in RUNS:
            scratch += [vmem((7, TOKENS, run[2] // 2), bf)] * 2
    scratch += [vmem((12, h, 2, HALF, 128), bf) for h in GROUPS]
    scratch += [vmem((8, 12, 2 * h, 128), bf) for h in GROUPS] * 2
    scratch += [vmem((64, CAP, 2 * h, 128), bf) for h in GROUPS]
    scratch += [vmem((8, 8, CAP, 2 * h, 128), bf) for h in GROUPS]
    dma = pltpu.SemaphoreType.DMA
    scratch += [
        dma((6,)),
        dma((2,)),
        dma((2,)),
        dma((2,)),
        dma((2, 8, 7)),
        dma((N_RUNS, 2)),
        dma((N_RUNS, 2, 7)),
        dma((N_GROUPS,)),
        dma((N_GROUPS,)),
        dma((N_GROUPS,)),
        dma((N_GROUPS,)),
    ]
    in_vmem = pl.BlockSpec(memory_space=pltpu.VMEM)
    anywhere = pl.BlockSpec(memory_space=pl.ANY)
    heads = GROUPS[0]
    result = pl.pallas_call(
        kernel,
        out_shape=jax.ShapeDtypeStruct((12, 8, N_GROUPS, 2 * heads, 128), bf),
        in_specs=[in_vmem] * 5 + [anywhere] * 5,
        out_specs=in_vmem,
        scratch_shapes=scratch,
        compiler_params=pltpu.CompilerParams(
            collective_id=0, has_side_effects=True, vmem_limit_bytes=56 * 2**20
        ),
    )(
        region_agents,
        new_counts,
        cache_lengths,
        frequency,
        new_rows.reshape(12, 2, HALF, 1024),
        query_weight,
        key_weight,
        value_weight,
        cache_keys,
        cache_values,
    )
    return result.reshape(12, 64, 2, HEAD_DIM).transpose(0, 2, 1, 3).reshape(12, 2, 8192)


def solution(mesh):
    placed = (
        P(("grp", "col"), None, "row"),
        P("row", "col"),
        P("row", "col"),
        P("row", "col"),
        P(("grp", "row"), None, "col"),
        P(("grp", "row"), None, "col"),
        P(),
        P(),
        P(),
    )
    return jax.shard_map(
        local, mesh=mesh, in_specs=placed, out_specs=P(("grp", "col"), "row", None), check_vma=False
    )
```

```python
import jax
import jax.numpy as jnp
import numpy as np
from jax import lax
from jax.experimental import pallas as pl
from jax.experimental.pallas import tpu as pltpu
from jax.sharding import PartitionSpec as P

HEAD_DIM = 128
SLOTS = 16
CAP = 3
rotary_base = 500000.0
floor_score = -1e30
MESH = pl.DeviceIdType.MESH
SEND, RECV, BACK, SEAT, LENS, CNTS, TABLE = 0, 24, 120, 312, 328, 344, 384

GROUPS = (4, 4)
N_GROUPS = len(GROUPS)
HALF = SLOTS // 2
TOKENS = 12 * HALF
RUNS = ((0, 0, 1280), (1, 0, 768), (1, 768, 512))
N_RUNS = len(RUNS)
PLUS, MINUS = 0, 1
MESSAGES = ((1, 4), (0, 3), (1, 3), (0, 2), (1, 2), (0, 1), (1, 1))
OFFSETS = (4, 3, -3, 2, -2, 1, -1, 0)


def message_index(direction, half, distance):
    long = 1 if half == direction else 0
    return MESSAGES.index((long, distance))


def whole_wait(ref, sem):
    pltpu.make_async_copy(ref, ref, sem).wait()


def kernel(*refs):
    refs = list(refs)
    take = lambda n: [refs.pop(0) for _ in range(n)]
    agents, some_counts, some_lengths, frequency, rows, wq, wk, wv, keys, values = take(10)
    (out,) = take(1)
    table, compact, idx, cosine, sine = take(5)
    outg, arrv0, arrv1, xg, wbuf, kbuf, vbuf, kn, vn = take(9)
    arrv = (arrv0, arrv1)
    sbuf = [take(2) for _ in range(N_RUNS)]
    rbuf = [take(2) for _ in range(N_RUNS)]
    qs, zs, zr, bo, inc = (take(N_GROUPS) for _ in range(5))
    local_sem, d_send, d_recv, ag_send, ag_recv, rs_send_sem, rs_recv, z_send, z_recv, b_send, b_recv = take(11)

    g = lax.axis_index("grp")
    r = lax.axis_index("row")
    c = lax.axis_index("col")
    me = g * 8 + c

    loads = [
        pltpu.make_async_copy(wk, wbuf.at[:, pl.ds(0, HEAD_DIM)], local_sem.at[0]),
        pltpu.make_async_copy(wv, wbuf.at[:, pl.ds(HEAD_DIM, HEAD_DIM)], local_sem.at[1]),
        pltpu.make_async_copy(wq, wbuf.at[:, pl.ds(2 * HEAD_DIM, 1024)], local_sem.at[2]),
        pltpu.make_async_copy(keys, kbuf, local_sem.at[3]),
        pltpu.make_async_copy(values, vbuf, local_sem.at[4]),
    ]
    for load in loads:
        load.start()

    barrier = pltpu.get_barrier_semaphore()
    for i in range(8):
        for o in range(8):
            if (i, o) != (0, 0):
                pl.semaphore_signal(
                    barrier, inc=1, device_id=(lax.rem(g + i, 8), r, lax.rem(c + o, 8)), device_id_type=MESH
                )
    for i in range(1, 8):
        pl.semaphore_signal(barrier, inc=1, device_id=(g, lax.rem(r + i, 8), c), device_id_type=MESH)

    ra, all_counts, all_lengths = (n[...].reshape(1, 768) for n in (agents, some_counts, some_lengths))
    flat = lax.broadcasted_iota(jnp.int32, (1, 768), 1)
    region = lax.shift_right_logical(flat * 5462, 16)
    within = flat - region * 12
    served = lax.shift_right_logical(ra * 683, 16)
    bucket = jnp.zeros((1, 768), jnp.int32)
    for d in range(1, 12):
        same = (pltpu.roll(served, d, 1) == served) & (within >= d)
        bucket = bucket + same.astype(jnp.int32)
    place = region * CAP + bucket
    seat = served * CAP + bucket

    def pick(count, chosen, offset, values, most):
        want = lax.broadcasted_iota(jnp.int32, (count, 768), 0) + offset
        hit = jnp.broadcast_to(chosen, (count, 768)) == want
        total = jnp.sum(jnp.where(hit, jnp.broadcast_to(values, (count, 768)), 0), axis=1, keepdims=True)
        return jnp.broadcast_to(jnp.clip(total, 0, most), (count, 128))

    table[SEND : SEND + 24] = pick(24, jnp.where(region == me, seat, -1), 0, within, 11)
    table[RECV : RECV + 96] = pick(96, ra, g * 96, place, 64 * CAP - 1)
    table[BACK : BACK + 192] = pick(192, jnp.where(served == g, place, -1), 0, ra - g * 96, 95)
    table[SEAT : SEAT + 16] = pick(16, flat, me * 12, seat, 8 * CAP - 1)
    table[LENS : LENS + 16] = pick(16, flat, g * 96 + r * 12, all_lengths, 512)
    table[CNTS : CNTS + 16] = pick(16, flat, g * 96 + r * 12, all_counts, SLOTS)
    table[CNTS + 16 : TABLE] = jnp.zeros((TABLE - CNTS - 16, 128), jnp.int32)
    square = table[...].reshape(3, 128, 128)
    diagonal = lax.broadcasted_iota(jnp.int32, (3, 128, 128), 1) == lax.broadcasted_iota(jnp.int32, (3, 128, 128), 2)
    compact[...] = jnp.sum(jnp.where(diagonal, square, 0), axis=1)
    to_scalars = pltpu.make_async_copy(compact, idx, local_sem.at[5])
    to_scalars.start()
    to_scalars.wait()

    def number(at):
        return idx[at // 128, at % 128] if isinstance(at, int) else idx[lax.div(at, 128), lax.rem(at, 128)]

    def fill(s, target_group):
        for k in range(CAP):
            j = number(SEND + target_group * CAP + k)
            row = rows[j, s]
            for cc in range(8):
                outg[s, target_group * 8 + cc, k] = row[:, cc * 128 : (cc + 1) * 128]

    order = (4, 3, 5, 2, 6, 1, 7, 0)
    fill(0, lax.rem(g + order[0], 8))
    pl.semaphore_wait(barrier, 70)

    def dispatch(s):
        for n, i in enumerate(order):
            tg = lax.rem(g + i, 8)
            if n and s == 0:
                fill(s, tg)
            for o in range(8):
                tc = lax.rem(c + o, 8)
                if (i, o) == (0, 0):
                    arrv[s][me] = outg[s, me]
                    continue
                pltpu.make_async_remote_copy(
                    src_ref=outg.at[s, tg * 8 + tc],
                    dst_ref=arrv[s].at[me],
                    send_sem=d_send.at[s],
                    recv_sem=d_recv.at[s],
                    device_id=(tg, r, tc),
                    device_id_type=MESH,
                ).start()

    def dispatch_wait(s):
        whole_wait(arrv[s].at[pl.ds(0, 63)], d_recv.at[s])

    dispatch(0)
    for i in order:
        fill(1, lax.rem(g + i, 8))

    slots = lax.broadcasted_iota(jnp.int32, (HALF, 128), 0)
    lanes = lax.broadcasted_iota(jnp.int32, (HALF, 128), 1)
    for s in range(2):
        for a in range(12):
            angle = (slots + (number(LENS + a) + s * HALF)).astype(jnp.float32) * frequency[...]
            cosine[s, a * HALF : (a + 1) * HALF] = jnp.cos(angle)
            turn = jnp.sin(angle)
            sine[s, a * HALF : (a + 1) * HALF] = jnp.where(lanes < 64, -turn, turn)

    x, p = lax.div(c, 2), lax.rem(c, 2)
    ahead = lax.rem(x + 1 + 2 * p, 4) * 2 + p
    behind = lax.rem(x + 3 + 2 * p, 4) * 2 + p
    far = lax.rem(x + 2, 4) * 2 + p
    sibling = c + 1 - 2 * p
    block_of = [lax.rem(r + o + 8, 8) for o in OFFSETS]

    def ag_copy(s, t, origin, target, kind):
        k = block_of[t]
        return pltpu.make_async_remote_copy(
            src_ref=xg.at[s, k, origin],
            dst_ref=xg.at[s, k, origin],
            send_sem=ag_send.at[s],
            recv_sem=ag_recv.at[s, t, kind],
            device_id=(g, r, target),
            device_id_type=MESH,
        )

    def ag_wait(s, t, kind):
        whole_wait(xg.at[s, block_of[t], c], ag_recv.at[s, t, kind])

    def land(s, k):
        for a in range(12):
            seat = number(RECV + k * 12 + a)
            xg[s, k, c, a] = arrv[s][lax.div(seat, CAP), lax.rem(seat, CAP)]

    def ag_start(s, *ts):
        for t in ts:
            land(s, block_of[t])
            ag_copy(s, t, c, ahead, 1).start()
            ag_copy(s, t, c, behind, 2).start()
            ag_copy(s, t, c, sibling, 0).start()

    def ag_direct(s, t):
        k = block_of[t]
        land(s, k)
        for i in (3, 4, 5, 2, 6, 7, 1):
            ag_copy(s, t, c, lax.rem(c + i, 8), 0).start()

    def ag_direct_wait(s, t):
        whole_wait(xg.at[s, block_of[t], pl.ds(0, 7)], ag_recv.at[s, t, 0])

    def ag_first(s, *ts):
        for t in ts:
            ag_wait(s, t, 1)
            ag_copy(s, t, behind, ahead, 3).start()
            ag_copy(s, t, behind, sibling, 4).start()
            ag_wait(s, t, 2)
            ag_copy(s, t, ahead, sibling, 5).start()

    def ag_second(s, *ts):
        for t in ts:
            ag_wait(s, t, 3)
            ag_copy(s, t, far, sibling, 6).start()

    def ag_finish(s, *ts):
        for t in ts:
            for kind in (0, 4, 5, 6):
                ag_wait(s, t, kind)

    def tokens(s, t):
        k = block_of[t]
        return jnp.concatenate([xg[s, k, cc].reshape(TOKENS, 128) for cc in range(8)], axis=1)

    up, down = lax.rem(r + 1, 8), lax.rem(r + 7, 8)
    toward = (up, down)

    def partial(run, half, t):
        s, first, width = RUNS[run]
        width = width // 2
        at = pl.ds(first + half * width, width)
        return jnp.dot(tokens(s, t), wbuf[:, at], preferred_element_type=jnp.float32)

    def rs_wait(run, direction, m):
        whole_wait(rbuf[run][direction].at[m], rs_recv.at[run, direction, m])

    def rs_dot(run, *ms):
        for m in ms:
            is_long, distance = MESSAGES[m]
            for direction in (PLUS, MINUS):
                half = direction if is_long else 1 - direction
                t = OFFSETS.index(distance if direction == PLUS or distance == 4 else -distance)
                sbuf[run][direction][m] = partial(run, half, t).astype(jnp.bfloat16)

    def rs_send(run, m):
        is_long, distance = MESSAGES[m]
        for direction in (PLUS, MINUS):
            if (is_long, distance + 1) in MESSAGES:
                before = MESSAGES.index((is_long, distance + 1))
                rs_wait(run, direction, before)
                total = sbuf[run][direction][m].astype(jnp.float32) + rbuf[run][direction][before].astype(jnp.float32)
                sbuf[run][direction][m] = total.astype(jnp.bfloat16)
            pltpu.make_async_remote_copy(
                src_ref=sbuf[run][direction].at[m],
                dst_ref=rbuf[run][direction].at[m],
                send_sem=rs_send_sem.at[run, direction],
                recv_sem=rs_recv.at[run, direction, m],
                device_id=(g, toward[direction], c),
                device_id_type=MESH,
            ).start()

    def rotate(u, s):
        return u * cosine[s] + pltpu.roll(u, 64, 1) * sine[s]

    def finish(run):
        s, first, width = RUNS[run]
        blocks = width // 256
        for half in (0, 1):
            own = partial(run, half, 7)
            for direction in (PLUS, MINUS):
                m = message_index(direction, half, 1)
                rs_wait(run, direction, m)
                own = own + rbuf[run][direction][m].astype(jnp.float32)
            for b in range(blocks):
                piece = own[:, b * 128 : (b + 1) * 128]
                head = first // 128 + half * blocks + b - 2
                if head == -2:
                    kn[:, s] = rotate(piece, s).astype(jnp.bfloat16).reshape(12, HALF, 128)
                elif head == -1:
                    vn[:, s] = piece.astype(jnp.bfloat16).reshape(12, HALF, 128)
                else:
                    gi, at = divmod(head, GROUPS[0])
                    qs[gi][:, at, s] = rotate(piece, s).astype(jnp.bfloat16).reshape(12, HALF, 128)

    def z_start(gi, part):
        some = pl.ds(part * 6, 6)
        for i in (4, 3, 5, 2, 6, 1, 7):
            other = lax.rem(r + i, 8)
            pltpu.make_async_remote_copy(
                src_ref=zs[gi].at[other, some],
                dst_ref=zr[gi].at[r, some],
                send_sem=z_send.at[gi],
                recv_sem=z_recv.at[gi],
                device_id=(g, other, c),
                device_id_type=MESH,
            ).start()
        zr[gi][r, some] = zs[gi][r, some]

    def attend(gi):
        heads = GROUPS[gi]
        n = heads * SLOTS
        scale = HEAD_DIM ** (-0.5) * float(np.log2(np.e))
        row_s = lax.broadcasted_iota(jnp.int32, (n, SLOTS), 0) % SLOTS
        col_t = lax.broadcasted_iota(jnp.int32, (n, SLOTS), 1)
        causal = col_t <= row_s
        place = lax.broadcasted_iota(jnp.int32, (n, 512), 1)
        slot = lax.broadcasted_iota(jnp.int32, (n, 128), 0) % SLOTS
        i = lax.broadcasted_iota(jnp.int32, (n, n), 0)
        j = lax.broadcasted_iota(jnp.int32, (n, n), 1)
        pair, rest = i // (2 * heads), i % (2 * heads)
        swap = ((rest // 2) * SLOTS + pair * 2 + rest % 2 == j).astype(jnp.float32).astype(jnp.bfloat16)
        last = (((1,), (1,)), ((), ()))

        def one(a, _):
            length, count = number(LENS + a), number(CNTS + a)
            q = qs[gi][a].reshape(n, 128)
            s1 = lax.dot_general(q, kbuf[a], last, preferred_element_type=jnp.float32) * scale
            s2 = lax.dot_general(q, kn[a].reshape(SLOTS, 128), last, preferred_element_type=jnp.float32) * scale
            s1 = jnp.where(place < length, s1, floor_score)
            s2 = jnp.where(causal & (col_t < count), s2, floor_score)
            top = jnp.maximum(jnp.max(s1, axis=1, keepdims=True), jnp.max(s2, axis=1, keepdims=True))
            p1, p2 = jnp.exp2(s1 - top), jnp.exp2(s2 - top)
            den = jnp.sum(p1, axis=1, keepdims=True) + jnp.sum(p2, axis=1, keepdims=True)
            mixed = jnp.dot(p1.astype(jnp.bfloat16), vbuf[a], preferred_element_type=jnp.float32)
            mixed = mixed + jnp.dot(p2.astype(jnp.bfloat16), vn[a].reshape(SLOTS, 128), preferred_element_type=jnp.float32)
            mixed = jnp.where(slot < count, mixed / den, 0.0).astype(jnp.bfloat16)
            swapped = jnp.dot(swap, mixed, preferred_element_type=jnp.float32).astype(jnp.bfloat16)
            zs[gi][:, a] = swapped.reshape(8, 2 * heads, 128)
            return 0

        for part in range(2):
            lax.fori_loop(part * 6, part * 6 + 6, one, 0, unroll=2)
            z_start(gi, part)

    def back_start(gi):
        whole_wait(zr[gi].at[pl.ds(0, 7)], z_recv.at[gi])
        for i in order:
            tg = lax.rem(g + i, 8)
            for o in range(8):
                tc = lax.rem(c + o, 8)
                target = tg * 8 + tc
                for k in range(CAP):
                    a = number(BACK + target * CAP + k)
                    bo[gi][target, k] = zr[gi][lax.div(a, 12), lax.rem(a, 12)]
                if (i, o) == (0, 0):
                    inc[gi][g, c] = bo[gi][target]
                    continue
                pltpu.make_async_remote_copy(
                    src_ref=bo[gi].at[target],
                    dst_ref=inc[gi].at[g, c],
                    send_sem=b_send.at[gi],
                    recv_sem=b_recv.at[gi],
                    device_id=(tg, r, tc),
                    device_id_type=MESH,
                ).start()

    def back_finish(gi):
        whole_wait(bo[gi].at[pl.ds(0, 63)], b_recv.at[gi])
        for j in range(12):
            seat_j = number(SEAT + j)
            out[j, :, gi] = inc[gi][lax.div(seat_j, CAP), :, lax.rem(seat_j, CAP)]

    dispatch_wait(0)
    ag_direct(0, 0)
    ag_start(0, 1, 2)
    dispatch(1)
    ag_start(0, 3, 4)
    for load in loads[:3]:
        load.wait()
    ag_direct_wait(0, 0)
    rs_dot(0, 0)
    rs_send(0, 0)
    ag_first(0, 1, 2)
    ag_start(0, 5, 6, 7)
    ag_second(0, 1, 2)
    ag_finish(0, 1, 2)
    rs_dot(0, 1)
    rs_send(0, 1)
    ag_first(0, 3, 4)
    rs_dot(0, 2)
    ag_second(0, 3, 4)
    ag_finish(0, 3, 4)
    rs_send(0, 2)
    rs_dot(0, 3)
    ag_first(0, 5, 6, 7)
    rs_send(0, 3)
    rs_dot(0, 4)
    ag_second(0, 5, 6, 7)
    dispatch_wait(1)
    ag_start(1, 0, 1, 2)
    rs_send(0, 4)
    ag_finish(0, 5, 6, 7)
    rs_dot(0, 5, 6)
    ag_start(1, 3, 4)
    ag_first(1, 0, 1, 2)
    rs_send(0, 5)
    ag_start(1, 5, 6, 7)
    ag_second(1, 0, 1, 2)
    ag_finish(1, 0)
    rs_dot(1, 0)
    rs_send(1, 0)
    rs_send(0, 6)
    ag_finish(1, 1, 2)
    rs_dot(1, 1)
    rs_send(1, 1)
    ag_first(1, 3, 4)
    rs_dot(2, 0)
    rs_dot(1, 2)
    rs_send(2, 0)
    ag_second(1, 3, 4)
    rs_send(1, 2)
    ag_first(1, 5, 6, 7)
    ag_finish(1, 3, 4)
    rs_dot(1, 3)
    rs_dot(2, 1)
    rs_send(1, 3)
    rs_send(2, 1)
    rs_dot(1, 4)
    ag_second(1, 5, 6, 7)
    for load in loads[3:]:
        load.wait()
    finish(0)
    rs_send(1, 4)
    ag_finish(1, 5, 6, 7)
    rs_dot(1, 5)
    rs_dot(2, 2)
    rs_send(1, 5)
    rs_send(2, 2)
    rs_dot(1, 6)
    rs_dot(2, 3)
    rs_send(1, 6)
    rs_send(2, 3)
    rs_dot(2, 4, 5, 6)
    rs_send(2, 4)
    finish(1)
    rs_send(2, 5)
    attend(0)
    rs_send(2, 6)
    back_start(0)
    finish(2)
    attend(1)
    back_finish(0)
    back_start(1)
    back_finish(1)

    for s in range(2):
        whole_wait(outg.at[s, pl.ds(0, 63)], d_send.at[s])
        whole_wait(xg.at[s, pl.ds(0, 7)], ag_send.at[s])
    for run in range(N_RUNS):
        for direction in (PLUS, MINUS):
            whole_wait(sbuf[run][direction], rs_send_sem.at[run, direction])
    for gi in range(N_GROUPS):
        whole_wait(zs[gi].at[pl.ds(0, 7)], z_send.at[gi])
        whole_wait(bo[gi].at[pl.ds(0, 63)], b_send.at[gi])


def local(
    new_rows,
    query_weight,
    key_weight,
    value_weight,
    cache_keys,
    cache_values,
    region_agents,
    new_counts,
    cache_lengths,
):
    half_frequency = rotary_base ** (-np.arange(64) * (2.0 / HEAD_DIM))
    frequency = jnp.asarray(np.tile(half_frequency, 2).astype(np.float32).reshape(1, 128))
    bf, vmem = jnp.bfloat16, pltpu.VMEM
    scratch = [
        vmem((TABLE, 128), jnp.int32),
        vmem((3, 128), jnp.int32),
        pltpu.SMEM((3, 128), jnp.int32),
        vmem((2, TOKENS, 128), jnp.float32),
        vmem((2, TOKENS, 128), jnp.float32),
        vmem((2, 64, CAP, HALF, 128), bf),
        vmem((64, CAP, HALF, 128), bf),
        vmem((64, CAP, HALF, 128), bf),
        vmem((2, 8, 8, 12, HALF, 128), bf),
        vmem((1024, 1280), bf),
        vmem((12, 512, 128), bf),
        vmem((12, 512, 128), bf),
        vmem((12, 2, HALF, 128), bf),
        vmem((12, 2, HALF, 128), bf),
    ]
    for _ in range(2):
        for run in RUNS:
            scratch += [vmem((7, TOKENS, run[2] // 2), bf)] * 2
    scratch += [vmem((12, h, 2, HALF, 128), bf) for h in GROUPS]
    scratch += [vmem((8, 12, 2 * h, 128), bf) for h in GROUPS] * 2
    scratch += [vmem((64, CAP, 2 * h, 128), bf) for h in GROUPS]
    scratch += [vmem((8, 8, CAP, 2 * h, 128), bf) for h in GROUPS]
    dma = pltpu.SemaphoreType.DMA
    scratch += [
        dma((6,)),
        dma((2,)),
        dma((2,)),
        dma((2,)),
        dma((2, 8, 7)),
        dma((N_RUNS, 2)),
        dma((N_RUNS, 2, 7)),
        dma((N_GROUPS,)),
        dma((N_GROUPS,)),
        dma((N_GROUPS,)),
        dma((N_GROUPS,)),
    ]
    in_vmem = pl.BlockSpec(memory_space=pltpu.VMEM)
    anywhere = pl.BlockSpec(memory_space=pl.ANY)
    heads = GROUPS[0]
    result = pl.pallas_call(
        kernel,
        out_shape=jax.ShapeDtypeStruct((12, 8, N_GROUPS, 2 * heads, 128), bf),
        in_specs=[in_vmem] * 5 + [anywhere] * 5,
        out_specs=in_vmem,
        scratch_shapes=scratch,
        compiler_params=pltpu.CompilerParams(
            collective_id=0, has_side_effects=True, vmem_limit_bytes=56 * 2**20
        ),
    )(
        region_agents,
        new_counts,
        cache_lengths,
        frequency,
        new_rows.reshape(12, 2, HALF, 1024),
        query_weight,
        key_weight,
        value_weight,
        cache_keys,
        cache_values,
    )
    return result.reshape(12, 64, 2, HEAD_DIM).transpose(0, 2, 1, 3).reshape(12, 2, 8192)


def solution(mesh):
    placed = (
        P(("grp", "col"), None, "row"),
        P("row", "col"),
        P("row", "col"),
        P("row", "col"),
        P(("grp", "row"), None, "col"),
        P(("grp", "row"), None, "col"),
        P(),
        P(),
        P(),
    )
    return jax.shard_map(
        local, mesh=mesh, in_specs=placed, out_specs=P(("grp", "col"), "row", None), check_vma=False
    )
```

```python
import jax
import jax.numpy as jnp
import numpy as np
from jax import lax
from jax.experimental import pallas as pl
from jax.experimental.pallas import tpu as pltpu
from jax.sharding import PartitionSpec as P

HEAD_DIM = 128
SLOTS = 16
CAP = 3
rotary_base = 500000.0
floor_score = -1e30
MESH = pl.DeviceIdType.MESH
SEND, RECV, BACK, SEAT, LENS, CNTS, TABLE = 0, 24, 120, 312, 328, 344, 384

N_GROUPS = 2
HEADS = 8
HALF = SLOTS // 2
TOKENS = 12 * HALF
RUNS = ((0, 0, 1280), (1, 0, 256), (1, 256, 1024))
N_RUNS = len(RUNS)
PLUS, MINUS = 0, 1
MESSAGES = ((1, 4), (0, 3), (1, 3), (0, 2), (1, 2), (0, 1), (1, 1))
OFFSETS = (4, 3, -3, 2, -2, 1, -1, 0)


def message_index(direction, half, distance):
    long = 1 if half == direction else 0
    return MESSAGES.index((long, distance))


def whole_wait(ref, sem):
    pltpu.make_async_copy(ref, ref, sem).wait()


def kernel(*refs):
    refs = list(refs)
    take = lambda n: [refs.pop(0) for _ in range(n)]
    agents, some_counts, some_lengths, frequency, rows, wq, wk, wv, keys, values = take(10)
    (out,) = take(1)
    table, compact, idx, cosine, sine = take(5)
    prow, outg, arrv0, arrv1, xg, wbuf, kbuf, vbuf, kn, vn = take(10)
    arrv = (arrv0, arrv1)
    sbuf = [take(2) for _ in range(N_RUNS)]
    rbuf = [take(2) for _ in range(N_RUNS)]
    qs, zs, zr, bo, inc = (take(N_GROUPS) for _ in range(5))
    local_sem, d_send, d_recv, ag_send, ag_recv, rs_send_sem, rs_recv, z_send, z_recv, b_send, b_recv = take(11)

    g = lax.axis_index("grp")
    r = lax.axis_index("row")
    c = lax.axis_index("col")
    me = g * 8 + c

    loads = [
        pltpu.make_async_copy(wk, wbuf.at[:, pl.ds(0, HEAD_DIM)], local_sem.at[0]),
        pltpu.make_async_copy(wv, wbuf.at[:, pl.ds(HEAD_DIM, HEAD_DIM)], local_sem.at[1]),
        pltpu.make_async_copy(wq, wbuf.at[:, pl.ds(2 * HEAD_DIM, 1024)], local_sem.at[2]),
        pltpu.make_async_copy(keys, kbuf, local_sem.at[3]),
        pltpu.make_async_copy(values, vbuf, local_sem.at[4]),
    ]
    for load in loads:
        load.start()

    barrier = pltpu.get_barrier_semaphore()
    for i in range(8):
        for o in range(8):
            if (i, o) != (0, 0):
                pl.semaphore_signal(
                    barrier, inc=1, device_id=(lax.rem(g + i, 8), r, lax.rem(c + o, 8)), device_id_type=MESH
                )
    for i in range(1, 8):
        pl.semaphore_signal(barrier, inc=1, device_id=(g, lax.rem(r + i, 8), c), device_id_type=MESH)

    ra, all_counts, all_lengths = (n[...].reshape(1, 768) for n in (agents, some_counts, some_lengths))
    flat = lax.broadcasted_iota(jnp.int32, (1, 768), 1)
    region = lax.shift_right_logical(flat * 5462, 16)
    within = flat - region * 12
    served = lax.shift_right_logical(ra * 683, 16)
    bucket = jnp.zeros((1, 768), jnp.int32)
    for d in range(1, 12):
        same = (pltpu.roll(served, d, 1) == served) & (within >= d)
        bucket = bucket + same.astype(jnp.int32)
    place = region * CAP + bucket
    seat = served * CAP + bucket

    def pick(count, chosen, offset, values, most):
        want = lax.broadcasted_iota(jnp.int32, (count, 768), 0) + offset
        hit = jnp.broadcast_to(chosen, (count, 768)) == want
        total = jnp.sum(jnp.where(hit, jnp.broadcast_to(values, (count, 768)), 0), axis=1, keepdims=True)
        return jnp.broadcast_to(jnp.clip(total, 0, most), (count, 128))

    table[SEND : SEND + 24] = pick(24, jnp.where(region == me, seat, -1), 0, within, 11)
    table[RECV : RECV + 96] = pick(96, ra, g * 96, place, 64 * CAP - 1)
    table[BACK : BACK + 192] = pick(192, jnp.where(served == g, place, -1), 0, ra - g * 96, 95)
    table[SEAT : SEAT + 16] = pick(16, flat, me * 12, seat, 8 * CAP - 1)
    table[LENS : LENS + 16] = pick(16, flat, g * 96 + r * 12, all_lengths, 512)
    table[CNTS : CNTS + 16] = pick(16, flat, g * 96 + r * 12, all_counts, SLOTS)
    table[CNTS + 16 : TABLE] = jnp.zeros((TABLE - CNTS - 16, 128), jnp.int32)
    square = table[...].reshape(3, 128, 128)
    diagonal = lax.broadcasted_iota(jnp.int32, (3, 128, 128), 1) == lax.broadcasted_iota(jnp.int32, (3, 128, 128), 2)
    compact[...] = jnp.sum(jnp.where(diagonal, square, 0), axis=1)
    to_scalars = pltpu.make_async_copy(compact, idx, local_sem.at[5])
    to_scalars.start()
    to_scalars.wait()

    to = lax.broadcasted_iota(jnp.int32, (SLOTS, SLOTS), 0)
    of = lax.broadcasted_iota(jnp.int32, (SLOTS, SLOTS), 1)
    apart = (2 * (to % HALF) + to // HALF == of).astype(jnp.float32).astype(jnp.bfloat16)
    for j in range(12):
        moved = jnp.dot(apart, rows[j], preferred_element_type=jnp.float32).astype(jnp.bfloat16)
        prow[j] = moved.reshape(2, HALF, 1024)

    def number(at):
        return idx[at // 128, at % 128] if isinstance(at, int) else idx[lax.div(at, 128), lax.rem(at, 128)]

    def fill(s, target_group):
        for k in range(CAP):
            j = number(SEND + target_group * CAP + k)
            row = prow[j, s]
            for cc in range(8):
                outg[s, target_group * 8 + cc, k] = row[:, cc * 128 : (cc + 1) * 128]

    order = (4, 3, 5, 2, 6, 1, 7, 0)
    fill(0, lax.rem(g + order[0], 8))
    pl.semaphore_wait(barrier, 70)

    def dispatch(s):
        for n, i in enumerate(order):
            tg = lax.rem(g + i, 8)
            if n and s == 0:
                fill(s, tg)
            for o in range(8):
                tc = lax.rem(c + o, 8)
                if (i, o) == (0, 0):
                    arrv[s][me] = outg[s, me]
                    continue
                pltpu.make_async_remote_copy(
                    src_ref=outg.at[s, tg * 8 + tc],
                    dst_ref=arrv[s].at[me],
                    send_sem=d_send.at[s],
                    recv_sem=d_recv.at[s],
                    device_id=(tg, r, tc),
                    device_id_type=MESH,
                ).start()

    def dispatch_wait(s):
        whole_wait(arrv[s].at[pl.ds(0, 63)], d_recv.at[s])

    dispatch(0)
    for i in order:
        fill(1, lax.rem(g + i, 8))

    slots = lax.broadcasted_iota(jnp.int32, (HALF, 128), 0)
    lanes = lax.broadcasted_iota(jnp.int32, (HALF, 128), 1)
    for s in range(2):
        for a in range(12):
            angle = (2 * slots + (number(LENS + a) + s)).astype(jnp.float32) * frequency[...]
            cosine[s, a * HALF : (a + 1) * HALF] = jnp.cos(angle)
            turn = jnp.sin(angle)
            sine[s, a * HALF : (a + 1) * HALF] = jnp.where(lanes < 64, -turn, turn)

    x, p = lax.div(c, 2), lax.rem(c, 2)
    ahead = lax.rem(x + 1 + 2 * p, 4) * 2 + p
    behind = lax.rem(x + 3 + 2 * p, 4) * 2 + p
    far = lax.rem(x + 2, 4) * 2 + p
    sibling = c + 1 - 2 * p
    block_of = [lax.rem(r + o + 8, 8) for o in OFFSETS]

    def ag_copy(s, t, origin, target, kind):
        k = block_of[t]
        return pltpu.make_async_remote_copy(
            src_ref=xg.at[s, k, origin],
            dst_ref=xg.at[s, k, origin],
            send_sem=ag_send.at[s],
            recv_sem=ag_recv.at[s, t, kind],
            device_id=(g, r, target),
            device_id_type=MESH,
        )

    def ag_wait(s, t, kind):
        whole_wait(xg.at[s, block_of[t], c], ag_recv.at[s, t, kind])

    def land(s, k):
        for a in range(12):
            seat = number(RECV + k * 12 + a)
            xg[s, k, c, a] = arrv[s][lax.div(seat, CAP), lax.rem(seat, CAP)]

    def ag_start(s, *ts):
        for t in ts:
            land(s, block_of[t])
            ag_copy(s, t, c, ahead, 1).start()
            ag_copy(s, t, c, behind, 2).start()
            ag_copy(s, t, c, sibling, 0).start()

    def ag_direct(s, t):
        k = block_of[t]
        land(s, k)
        for i in (3, 4, 5, 2, 6, 7, 1):
            ag_copy(s, t, c, lax.rem(c + i, 8), 0).start()

    def ag_direct_wait(s, t):
        whole_wait(xg.at[s, block_of[t], pl.ds(0, 7)], ag_recv.at[s, t, 0])

    def ag_first(s, *ts):
        for t in ts:
            ag_wait(s, t, 1)
            ag_copy(s, t, behind, ahead, 3).start()
            ag_copy(s, t, behind, sibling, 4).start()
            ag_wait(s, t, 2)
            ag_copy(s, t, ahead, sibling, 5).start()

    def ag_second(s, *ts):
        for t in ts:
            ag_wait(s, t, 3)
            ag_copy(s, t, far, sibling, 6).start()

    def ag_finish(s, *ts):
        for t in ts:
            for kind in (0, 4, 5, 6):
                ag_wait(s, t, kind)

    def tokens(s, t):
        k = block_of[t]
        return jnp.concatenate([xg[s, k, cc].reshape(TOKENS, 128) for cc in range(8)], axis=1)

    up, down = lax.rem(r + 1, 8), lax.rem(r + 7, 8)
    toward = (up, down)

    def partial(run, half, t):
        s, first, width = RUNS[run]
        width = width // 2
        at = pl.ds(first + half * width, width)
        return jnp.dot(tokens(s, t), wbuf[:, at], preferred_element_type=jnp.float32)

    def rs_wait(run, direction, m):
        whole_wait(rbuf[run][direction].at[m], rs_recv.at[run, direction, m])

    def rs_dot(run, *ms):
        for m in ms:
            is_long, distance = MESSAGES[m]
            for direction in (PLUS, MINUS):
                half = direction if is_long else 1 - direction
                t = OFFSETS.index(distance if direction == PLUS or distance == 4 else -distance)
                sbuf[run][direction][m] = partial(run, half, t).astype(jnp.bfloat16)

    def rs_send(run, m):
        is_long, distance = MESSAGES[m]
        for direction in (PLUS, MINUS):
            if (is_long, distance + 1) in MESSAGES:
                before = MESSAGES.index((is_long, distance + 1))
                rs_wait(run, direction, before)
                total = sbuf[run][direction][m].astype(jnp.float32) + rbuf[run][direction][before].astype(jnp.float32)
                sbuf[run][direction][m] = total.astype(jnp.bfloat16)
            pltpu.make_async_remote_copy(
                src_ref=sbuf[run][direction].at[m],
                dst_ref=rbuf[run][direction].at[m],
                send_sem=rs_send_sem.at[run, direction],
                recv_sem=rs_recv.at[run, direction, m],
                device_id=(g, toward[direction], c),
                device_id_type=MESH,
            ).start()

    def rotate(u, s):
        return u * cosine[s] + pltpu.roll(u, 64, 1) * sine[s]

    def finish(run):
        s, first, width = RUNS[run]
        blocks = width // 256
        for half in (0, 1):
            own = partial(run, half, 7)
            for direction in (PLUS, MINUS):
                m = message_index(direction, half, 1)
                rs_wait(run, direction, m)
                own = own + rbuf[run][direction][m].astype(jnp.float32)
            for b in range(blocks):
                piece = own[:, b * 128 : (b + 1) * 128]
                head = first // 128 + half * blocks + b - 2
                if head == -2:
                    kn[:, s] = rotate(piece, s).astype(jnp.bfloat16).reshape(12, HALF, 128)
                elif head == -1:
                    vn[:, s] = piece.astype(jnp.bfloat16).reshape(12, HALF, 128)
                else:
                    qs[s][:, head] = rotate(piece, s).astype(jnp.bfloat16).reshape(12, HALF, 128)

    def z_start(gi, part):
        some = pl.ds(part * 6, 6)
        for i in (4, 3, 5, 2, 6, 1, 7):
            other = lax.rem(r + i, 8)
            pltpu.make_async_remote_copy(
                src_ref=zs[gi].at[other, some],
                dst_ref=zr[gi].at[r, some],
                send_sem=z_send.at[gi],
                recv_sem=z_recv.at[gi],
                device_id=(g, other, c),
                device_id_type=MESH,
            ).start()
        zr[gi][r, some] = zs[gi][r, some]

    def attend(gi, *parts):
        n = HEADS * HALF
        scale = HEAD_DIM ** (-0.5) * float(np.log2(np.e))
        row_s = 2 * (lax.broadcasted_iota(jnp.int32, (n, SLOTS), 0) % HALF) + gi
        col_t = lax.broadcasted_iota(jnp.int32, (n, SLOTS), 1)
        col_t = 2 * (col_t % HALF) + col_t // HALF
        causal = col_t <= row_s
        place = lax.broadcasted_iota(jnp.int32, (n, 512), 1)
        slot = 2 * (lax.broadcasted_iota(jnp.int32, (n, 128), 0) % HALF) + gi
        i = lax.broadcasted_iota(jnp.int32, (n, n), 0)
        j = lax.broadcasted_iota(jnp.int32, (n, n), 1)
        swap = ((i % HEADS) * HALF + i // HEADS == j).astype(jnp.float32).astype(jnp.bfloat16)
        last = (((1,), (1,)), ((), ()))

        def one(a, _):
            length, count = number(LENS + a), number(CNTS + a)
            q = qs[gi][a].reshape(n, 128)
            s1 = lax.dot_general(q, kbuf[a], last, preferred_element_type=jnp.float32) * scale
            s2 = lax.dot_general(q, kn[a].reshape(SLOTS, 128), last, preferred_element_type=jnp.float32) * scale
            s1 = jnp.where(place < length, s1, floor_score)
            s2 = jnp.where(causal & (col_t < count), s2, floor_score)
            top = jnp.maximum(jnp.max(s1, axis=1, keepdims=True), jnp.max(s2, axis=1, keepdims=True))
            p1, p2 = jnp.exp2(s1 - top), jnp.exp2(s2 - top)
            den = jnp.sum(p1, axis=1, keepdims=True) + jnp.sum(p2, axis=1, keepdims=True)
            mixed = jnp.dot(p1.astype(jnp.bfloat16), vbuf[a], preferred_element_type=jnp.float32)
            mixed = mixed + jnp.dot(p2.astype(jnp.bfloat16), vn[a].reshape(SLOTS, 128), preferred_element_type=jnp.float32)
            mixed = jnp.where(slot < count, mixed / den, 0.0).astype(jnp.bfloat16)
            swapped = jnp.dot(swap, mixed, preferred_element_type=jnp.float32).astype(jnp.bfloat16)
            zs[gi][:, a] = swapped.reshape(8, HEADS, 128)
            return 0

        for part in parts:
            lax.fori_loop(part * 6, part * 6 + 6, one, 0, unroll=2)
            z_start(gi, part)

    def back_start(gi):
        whole_wait(zr[gi].at[pl.ds(0, 7)], z_recv.at[gi])
        for i in order:
            tg = lax.rem(g + i, 8)
            for o in range(8):
                tc = lax.rem(c + o, 8)
                target = tg * 8 + tc
                for k in range(CAP):
                    a = number(BACK + target * CAP + k)
                    bo[gi][target, k] = zr[gi][lax.div(a, 12), lax.rem(a, 12)]
                if (i, o) == (0, 0):
                    inc[gi][g, c] = bo[gi][target]
                    continue
                pltpu.make_async_remote_copy(
                    src_ref=bo[gi].at[target],
                    dst_ref=inc[gi].at[g, c],
                    send_sem=b_send.at[gi],
                    recv_sem=b_recv.at[gi],
                    device_id=(tg, r, tc),
                    device_id_type=MESH,
                ).start()

    def back_finish(gi):
        whole_wait(bo[gi].at[pl.ds(0, 63)], b_recv.at[gi])
        for j in range(12):
            seat_j = number(SEAT + j)
            out[j, :, gi] = inc[gi][lax.div(seat_j, CAP), :, lax.rem(seat_j, CAP)]

    dispatch_wait(0)
    ag_direct(0, 0)
    ag_start(0, 1, 2)
    dispatch(1)
    ag_start(0, 3, 4)
    for load in loads[:3]:
        load.wait()
    ag_direct_wait(0, 0)
    rs_dot(0, 0)
    rs_send(0, 0)
    ag_first(0, 1, 2)
    ag_start(0, 5, 6, 7)
    ag_second(0, 1, 2)
    ag_finish(0, 1, 2)
    rs_dot(0, 1)
    rs_send(0, 1)
    ag_first(0, 3, 4)
    rs_dot(0, 2)
    ag_second(0, 3, 4)
    ag_finish(0, 3, 4)
    rs_send(0, 2)
    rs_dot(0, 3)
    ag_first(0, 5, 6, 7)
    rs_send(0, 3)
    rs_dot(0, 4)
    ag_second(0, 5, 6, 7)
    dispatch_wait(1)
    ag_start(1, 0, 1, 2)
    rs_send(0, 4)
    ag_finish(0, 5, 6, 7)
    rs_dot(0, 5, 6)
    ag_start(1, 3, 4)
    ag_first(1, 0, 1, 2)
    rs_send(0, 5)
    ag_start(1, 5, 6, 7)
    ag_second(1, 0, 1, 2)
    ag_finish(1, 0)
    rs_dot(1, 0)
    rs_send(1, 0)
    rs_send(0, 6)
    rs_dot(2, 0)
    ag_finish(1, 1, 2)
    rs_dot(1, 1)
    rs_send(1, 1)
    rs_send(2, 0)
    rs_dot(1, 2)
    ag_first(1, 3, 4)
    rs_send(1, 2)
    rs_dot(2, 1)
    rs_send(2, 1)
    ag_second(1, 3, 4)
    ag_first(1, 5, 6, 7)
    ag_finish(1, 3, 4)
    rs_dot(1, 3, 4)
    rs_send(1, 3)
    rs_dot(2, 2)
    ag_second(1, 5, 6, 7)
    for load in loads[3:]:
        load.wait()
    rs_send(1, 4)
    rs_send(2, 2)
    ag_finish(1, 5, 6, 7)
    rs_dot(1, 5, 6)
    rs_send(1, 5)
    rs_dot(2, 3)
    rs_send(1, 6)
    rs_send(2, 3)
    finish(0)
    rs_dot(2, 4)
    rs_send(2, 4)
    finish(1)
    rs_dot(2, 5, 6)
    attend(0, 0)
    rs_send(2, 5)
    attend(0, 1)
    rs_send(2, 6)
    back_start(0)
    finish(2)
    attend(1, 0, 1)
    back_finish(0)
    back_start(1)
    back_finish(1)

    for s in range(2):
        whole_wait(outg.at[s, pl.ds(0, 63)], d_send.at[s])
        whole_wait(xg.at[s, pl.ds(0, 7)], ag_send.at[s])
    for run in range(N_RUNS):
        for direction in (PLUS, MINUS):
            whole_wait(sbuf[run][direction], rs_send_sem.at[run, direction])
    for gi in range(N_GROUPS):
        whole_wait(zs[gi].at[pl.ds(0, 7)], z_send.at[gi])
        whole_wait(bo[gi].at[pl.ds(0, 63)], b_send.at[gi])


def local(
    new_rows,
    query_weight,
    key_weight,
    value_weight,
    cache_keys,
    cache_values,
    region_agents,
    new_counts,
    cache_lengths,
):
    half_frequency = rotary_base ** (-np.arange(64) * (2.0 / HEAD_DIM))
    frequency = jnp.asarray(np.tile(half_frequency, 2).astype(np.float32).reshape(1, 128))
    bf, vmem = jnp.bfloat16, pltpu.VMEM
    scratch = [
        vmem((TABLE, 128), jnp.int32),
        vmem((3, 128), jnp.int32),
        pltpu.SMEM((3, 128), jnp.int32),
        vmem((2, TOKENS, 128), jnp.float32),
        vmem((2, TOKENS, 128), jnp.float32),
        vmem((12, 2, HALF, 1024), bf),
        vmem((2, 64, CAP, HALF, 128), bf),
        vmem((64, CAP, HALF, 128), bf),
        vmem((64, CAP, HALF, 128), bf),
        vmem((2, 8, 8, 12, HALF, 128), bf),
        vmem((1024, 1280), bf),
        vmem((12, 512, 128), bf),
        vmem((12, 512, 128), bf),
        vmem((12, 2, HALF, 128), bf),
        vmem((12, 2, HALF, 128), bf),
    ]
    for _ in range(2):
        for run in RUNS:
            scratch += [vmem((7, TOKENS, run[2] // 2), bf)] * 2
    scratch += [vmem((12, HEADS, HALF, 128), bf)] * 2
    scratch += [vmem((8, 12, HEADS, 128), bf)] * 4
    scratch += [vmem((64, CAP, HEADS, 128), bf)] * 2
    scratch += [vmem((8, 8, CAP, HEADS, 128), bf)] * 2
    dma = pltpu.SemaphoreType.DMA
    scratch += [
        dma((6,)),
        dma((2,)),
        dma((2,)),
        dma((2,)),
        dma((2, 8, 7)),
        dma((N_RUNS, 2)),
        dma((N_RUNS, 2, 7)),
        dma((N_GROUPS,)),
        dma((N_GROUPS,)),
        dma((N_GROUPS,)),
        dma((N_GROUPS,)),
    ]
    in_vmem = pl.BlockSpec(memory_space=pltpu.VMEM)
    anywhere = pl.BlockSpec(memory_space=pl.ANY)
    result = pl.pallas_call(
        kernel,
        out_shape=jax.ShapeDtypeStruct((12, 8, 2, HEADS, 128), bf),
        in_specs=[in_vmem] * 5 + [anywhere] * 5,
        out_specs=in_vmem,
        scratch_shapes=scratch,
        compiler_params=pltpu.CompilerParams(
            collective_id=0, has_side_effects=True, vmem_limit_bytes=56 * 2**20
        ),
    )(
        region_agents,
        new_counts,
        cache_lengths,
        frequency,
        new_rows,
        query_weight,
        key_weight,
        value_weight,
        cache_keys,
        cache_values,
    )
    return result.transpose(0, 2, 1, 3, 4).reshape(12, 2, 8192)


def solution(mesh):
    placed = (
        P(("grp", "col"), None, "row"),
        P("row", "col"),
        P("row", "col"),
        P("row", "col"),
        P(("grp", "row"), None, "col"),
        P(("grp", "row"), None, "col"),
        P(),
        P(),
        P(),
    )
    return jax.shard_map(
        local, mesh=mesh, in_specs=placed, out_specs=P(("grp", "col"), "row", None), check_vma=False
    )
```
